128 devices in a mesh: seq: 32 (over z, y, core), rep: 4 (over x).
Axes of the slice: x: 4, y: 4, z: 4, core: 2. Of those that a mesh axis runs over, the one named last changes fastest.
Arguments:
- queries: bfloat16 [4, 8192, 512], P('rep', 'seq'), may hold values from -6 to 6
- key_vectors: bfloat16 [4, 8192, 128], P('rep', 'seq'), may hold values from -6 to 6
- values: bfloat16 [4, 8192, 128], P('rep', 'seq'), may hold values from -6 to 6
- forget_logit: bfloat16 [4, 4, 8192], P('rep', None, 'seq'), may hold values from 0 to 11
- out_grad: bfloat16 [4, 8192, 512], P('rep', 'seq'), may hold values from -6 to 6
- query_gain: float32 [128], replicated, may hold values from 0.1 to 1.9
- key_gain: float32 [128], replicated, may hold values from 0.1 to 1.9
- lengths: int32 [4, 4], P('rep'), may hold values from 1 to 96, 128 in all within a row
Outputs:
- attention: bfloat16 [4, 8192, 512], P('rep', 'seq')
- query_grad: bfloat16 [4, 8192, 512], P('rep', 'seq')
- key_grad: bfloat16 [4, 8192, 128], P('rep', 'seq')
- value_grad: bfloat16 [4, 8192, 128], P('rep', 'seq')
- forget_grad: float32 [4, 4, 8192], P('rep', None, 'seq')
- norm_gain_grad: float32 [2, 128], replicated
The draws below stay inside these ranges and needn't reach their ends.
Inputs may be any that keep to these rules, and one draw needn't show every extreme that they name: `lengths`: each row lists the documents of one pack in order, in tiles of 64 tokens, and sums to 128.
All inputs are finite; a program needn't handle non-finite values.
Results may differ from the reference program's by a relative error of at most 0.02.
Values may be sent and summed in bfloat16 or wider, within the bound.
A program may use at most 64 MiB of HBM per device.

```python
import math
import jax
import jax.numpy as jnp
import numpy as np
from jax import lax

QUERY_HEAD_GROUP = 4
DH = 128
TILE = 64
TILE_DEV = 4
PACK_TOTAL = 4
SERVERS = 32
TOK_DEV = 256
TOKENS_PER_PACK = 8192
TILES = 128
DOCS = 4
DOC_MOST = 96


def draw_forget_logit(key, part):
    random_split_keys = jax.random.split(key, 5)
    chain_length = DOC_MOST * TILE * 1.0
    head_keys = jax.random.split(random_split_keys[0], PACK_TOTAL)
    head_order = jax.vmap(lambda head_key: jax.random.permutation(head_key, QUERY_HEAD_GROUP))(head_keys)
    is_slow = head_order >= QUERY_HEAD_GROUP // 2
    base_rate = jnp.where(is_slow, 1.0 / chain_length, 1.0 / 40.0)[:, :, None]
    roughness = jnp.exp(jax.random.uniform(random_split_keys[1], (PACK_TOTAL, QUERY_HEAD_GROUP, TOKENS_PER_PACK), minval=-0.7, maxval=0.7))
    block_total = TOKENS_PER_PACK // TOK_DEV
    device_scale = jnp.exp(jax.random.uniform(random_split_keys[2], (PACK_TOTAL, QUERY_HEAD_GROUP, block_total, 1), minval=-0.7, maxval=0.7))
    device_scale = jnp.broadcast_to(device_scale, (PACK_TOTAL, QUERY_HEAD_GROUP, block_total, TOK_DEV)).reshape(PACK_TOTAL, QUERY_HEAD_GROUP, TOKENS_PER_PACK)
    forget_decay_rate = base_rate * roughness * device_scale
    spike_mask = jax.random.uniform(random_split_keys[3], (PACK_TOTAL, QUERY_HEAD_GROUP, TOKENS_PER_PACK)) < 6.0 / TOKENS_PER_PACK
    spike_rate = jax.random.uniform(random_split_keys[4], (PACK_TOTAL, QUERY_HEAD_GROUP, TOKENS_PER_PACK), minval=0.22, maxval=0.69)
    forget_decay_rate = jnp.where(spike_mask, spike_rate, forget_decay_rate)
    return (-jnp.log(jnp.expm1(forget_decay_rate))).astype(jnp.float32).astype(jnp.bfloat16)


def block_levels(rng, dims, cuts, least, high):
    loudness, own = 1.0, jax.random.fold_in(rng, 6)
    for axis_at, blocks in cuts:
        heights = jnp.exp(jax.random.uniform(jax.random.fold_in(own, axis_at), (blocks,), jnp.float32, least / len(cuts), high / len(cuts)))
        loudness = loudness * jnp.repeat(heights, dims[axis_at] // blocks).reshape([-1 if axis == axis_at else 1 for axis in range(len(dims))])
    return loudness


def profile(number_of, total, bound, slope):
    weights = [(1 << 20) // math.isqrt(rank ** slope) + 1 for rank in range(2, number_of + 1)]
    rest, holding = total - bound - (number_of - 1), [1] * (number_of - 1)
    while rest > 0:
        movable = [i for i in range(number_of - 1) if holding[i] < bound]
        pool, left = sum([weights[i] for i in movable]), rest
        for i in movable:
            more = min(bound - holding[i], max(1, left * weights[i] // pool), rest)
            holding[i] = holding[i] + more
            rest = rest - more
    return np.array([bound] + holding)


def ragged_sizes(key, amount, total, bound, skew):
    if amount == 2:
        one = jax.random.randint(key, (), max(1, total - bound), min(bound, total - 1) + 1)
        return jnp.stack([one, total - one])
    tallies = jnp.asarray(profile(amount, total, bound, skew), jnp.int32)
    twos = (amount - 1) // 2
    source_of, receiver = tallies[1:1 + 2 * twos:2], tallies[2:2 + 2 * twos:2]
    room = jnp.minimum(source_of - 1, bound - receiver)
    moved = jax.random.randint(jax.random.fold_in(key, 1), (twos,), 0, 1 << 20) % (room + 1)
    tallies = tallies.at[1:1 + 2 * twos:2].set(source_of - moved).at[2:2 + 2 * twos:2].set(receiver + moved)
    return tallies[jax.random.permutation(jax.random.fold_in(key, 2), amount)]


def normal_values(stream_key, shape, deviation, bound, cuts=(), kind=jnp.bfloat16):
    values = jax.random.normal(stream_key, shape, jnp.float32) * deviation
    if len(cuts) > 0:
        values = block_levels(stream_key, shape, cuts, -0.22, 0.18) * values
    return jnp.clip(values, min=-bound, max=bound).astype(kind)


def setup_inputs(seed: int = 0) -> dict:
    keys = jax.random.split(jax.random.key(seed), 9)
    queries = normal_values(keys[0], (PACK_TOTAL, TOKENS_PER_PACK, QUERY_HEAD_GROUP * DH), 1.0, 6.0, ((0, 4), (1, 32)))
    key_vectors = normal_values(keys[1], (PACK_TOTAL, TOKENS_PER_PACK, DH), 1.0, 6.0, ((0, 4), (1, 32)))
    values = normal_values(keys[2], (PACK_TOTAL, TOKENS_PER_PACK, DH), 1.0, 6.0, ((0, 4), (1, 32)))
    forget_logit = draw_forget_logit(jax.random.fold_in(keys[8], 71), 0)
    out_grad = normal_values(keys[4], (PACK_TOTAL, TOKENS_PER_PACK, QUERY_HEAD_GROUP * DH), 1.0, 6.0, ((0, 4), (1, 32)))
    query_gain = jnp.clip(1.0 + 0.18 * jax.random.normal(keys[5], (DH,), jnp.float32), 0.1, 1.9)
    key_gain = jnp.clip(1.0 + 0.18 * jax.random.normal(keys[6], (DH,), jnp.float32), 0.1, 1.9)
    lengths = jax.vmap(lambda own: ragged_sizes(own, DOCS, TILES, DOC_MOST, 2))(jax.random.split(keys[7], PACK_TOTAL)).reshape((PACK_TOTAL, DOCS)).astype(jnp.int32)
    return dict(queries=queries, key_vectors=key_vectors, values=values, forget_logit=forget_logit, out_grad=out_grad, query_gain=query_gain, key_gain=key_gain, lengths=lengths)


norm_eps = 1e-06
key_span = 512

def norm_rows(raw_values, gain_vec, factor):
    lifted = raw_values.astype(jnp.float32)
    mean_square = lax.optimization_barrier(jnp.mean(lifted * lifted, axis=-1, keepdims=True))
    return lifted * lax.rsqrt(mean_square + norm_eps) * (gain_vec * factor)

def tile_starts(lengths_row, tile_count):
    doc_ends = jnp.cumsum(lengths_row).astype(jnp.int32)
    tile_index = jnp.arange(tile_count, dtype=jnp.int32)
    passed = doc_ends[None, :] <= tile_index[:, None]
    return lax.optimization_barrier(jnp.sum(jnp.where(passed, lengths_row[None, :], 0), axis=1)).astype(jnp.int32)

def pad_rows(array_in, along):
    widths = [(0, 0)] * array_in.ndim
    widths[along] = (0, key_span)
    return jnp.pad(array_in, widths)

def block_scores(query_rows, key_pad, gate_pad, query_gate, block_first, tile_first, doc_first, head_count):
    key_block = lax.dynamic_slice_in_dim(key_pad, block_first, key_span, 0)
    scores = jnp.dot(query_rows, key_block.T, preferred_element_type=jnp.float32)
    row_count = query_rows.shape[0] // head_count
    scores = scores.reshape(head_count, row_count, key_span)
    key_gate = lax.dynamic_slice_in_dim(gate_pad, block_first, key_span, 1)
    scores = scores + query_gate[:, :, None] - key_gate[:, None, :]
    key_place = block_first + jnp.arange(key_span, dtype=jnp.int32)
    query_place = tile_first + jnp.arange(row_count, dtype=jnp.int32)
    allowed = (key_place[None, :] >= doc_first) & (key_place[None, :] <= query_place[:, None])
    return (jnp.where(allowed[None, :, :], scores, -jnp.inf), key_block)

def query_setup(query_tile, tile_id, doc_tile, gate_pad, query_gain, head_count, head_dim):
    row_count = query_tile.shape[0]
    scale_factor = head_dim ** (-0.5)
    normed = norm_rows(query_tile.reshape(row_count, head_count, head_dim), query_gain, scale_factor).astype(jnp.bfloat16)
    query_rows = normed.transpose(1, 0, 2).reshape(head_count * row_count, head_dim)
    tile_first = tile_id * row_count
    doc_first = doc_tile * row_count
    query_gate = lax.dynamic_slice_in_dim(gate_pad, tile_first, row_count, 1)
    block_count = (tile_first + row_count - doc_first + key_span - 1) // key_span
    return (query_rows, tile_first, doc_first, query_gate, block_count)

def forward_task(query_tile, tile_id, doc_tile, key_pad, value_pad, gate_pad, query_gain, head_count):
    row_count, full_width = query_tile.shape
    head_dim = key_pad.shape[1]
    query_rows, tile_first, doc_first, query_gate, block_count = query_setup(query_tile, tile_id, doc_tile, gate_pad, query_gain, head_count, head_dim)

    def block_step(block_index, loop_state):
        row_total, value_sum = loop_state
        block_first = doc_first + block_index * key_span
        scores, key_block = block_scores(query_rows, key_pad, gate_pad, query_gate, block_first, tile_first, doc_first, head_count)
        weights = jnp.exp(scores)
        value_block = lax.dynamic_slice_in_dim(value_pad, block_first, key_span, 0)
        mixed_rows = jnp.dot(weights.reshape(head_count * row_count, key_span).astype(jnp.bfloat16), value_block, preferred_element_type=jnp.float32)
        return (row_total + lax.optimization_barrier(jnp.sum(weights, axis=2)), value_sum + mixed_rows)
    start_state = (jnp.zeros((head_count, row_count), jnp.float32), jnp.zeros((head_count * row_count, head_dim), jnp.float32))
    row_total, value_sum = lax.fori_loop(0, block_count, block_step, start_state)
    result = value_sum.reshape(head_count, row_count, head_dim) / row_total[:, :, None]
    return result.transpose(1, 0, 2).reshape(row_count, full_width).astype(jnp.bfloat16)

def backward_task(partials, query_tile, grad_tile, out_tile, tile_id, doc_tile, key_pad, value_pad, gate_pad, query_gain, head_count):
    row_count, full_width = query_tile.shape
    head_dim = key_pad.shape[1]
    query_rows, tile_first, doc_first, query_gate, block_count = query_setup(query_tile, tile_id, doc_tile, gate_pad, query_gain, head_count, head_dim)
    grad_rows = grad_tile.reshape(row_count, head_count, head_dim).transpose(1, 0, 2).reshape(head_count * row_count, head_dim)
    product = grad_tile.astype(jnp.float32) * out_tile.astype(jnp.float32)
    out_inner = lax.optimization_barrier(jnp.sum(product.reshape(row_count, head_count, head_dim), axis=2)).T

    def total_step(block_index, row_total):
        block_first = doc_first + block_index * key_span
        scores, key_block = block_scores(query_rows, key_pad, gate_pad, query_gate, block_first, tile_first, doc_first, head_count)
        return row_total + lax.optimization_barrier(jnp.sum(jnp.exp(scores), axis=2))
    row_total = lax.fori_loop(0, block_count, total_step, jnp.zeros((head_count, row_count), jnp.float32))

    def grad_step(block_index, loop_state):
        key_part, value_part, gate_part, query_grad, row_sum = loop_state
        block_first = doc_first + block_index * key_span
        scores, key_block = block_scores(query_rows, key_pad, gate_pad, query_gate, block_first, tile_first, doc_first, head_count)
        probability = jnp.exp(scores) / row_total[:, :, None]
        value_block = lax.dynamic_slice_in_dim(value_pad, block_first, key_span, 0)
        prob_grad = jnp.dot(grad_rows, value_block.T, preferred_element_type=jnp.float32).reshape(head_count, row_count, key_span)
        score_grad = probability * (prob_grad - out_inner[:, :, None])
        score_low = score_grad.reshape(head_count * row_count, key_span).astype(jnp.bfloat16)
        prob_low = probability.reshape(head_count * row_count, key_span).astype(jnp.bfloat16)
        query_grad = query_grad + jnp.dot(score_low, key_block, preferred_element_type=jnp.float32)
        key_update = jnp.dot(score_low.T, query_rows, preferred_element_type=jnp.float32)
        value_update = jnp.dot(prob_low.T, grad_rows, preferred_element_type=jnp.float32)
        key_part = lax.dynamic_update_slice_in_dim(key_part, lax.dynamic_slice_in_dim(key_part, block_first, key_span, 0) + key_update, block_first, 0)
        value_part = lax.dynamic_update_slice_in_dim(value_part, lax.dynamic_slice_in_dim(value_part, block_first, key_span, 0) + value_update, block_first, 0)
        column_sum = lax.optimization_barrier(jnp.sum(score_grad, axis=1))
        gate_part = lax.dynamic_update_slice_in_dim(gate_part, lax.dynamic_slice_in_dim(gate_part, block_first, key_span, 1) - column_sum, block_first, 1)
        return (key_part, value_part, gate_part, query_grad, row_sum + lax.optimization_barrier(jnp.sum(score_grad, axis=2)))
    start_state = (partials[0], partials[1], partials[2], jnp.zeros((head_count * row_count, head_dim), jnp.float32), jnp.zeros((head_count, row_count), jnp.float32))
    key_part, value_part, gate_part, query_grad, row_sum = lax.fori_loop(0, block_count, grad_step, start_state)
    gate_part = lax.dynamic_update_slice_in_dim(gate_part, lax.dynamic_slice_in_dim(gate_part, tile_first, row_count, 1) + row_sum, tile_first, 1)
    query_result = query_grad.reshape(head_count, row_count, head_dim).transpose(1, 0, 2).reshape(row_count, full_width).astype(jnp.bfloat16)
    return ((key_part, value_part, gate_part), query_result)

def one_pack(query_local, key_local, value_local, logit_local, grad_local, query_gain, key_gain, lengths_row):
    token_count, full_width = query_local.shape
    head_dim = key_local.shape[1]
    head_count = full_width // head_dim
    tile_count = token_count // TILE
    key_normed = norm_rows(key_local, key_gain, 1.0).astype(jnp.bfloat16)
    gate = jnp.cumsum(jax.nn.log_sigmoid(logit_local.astype(jnp.float32)), axis=1)
    key_pad = pad_rows(key_normed, 0)
    value_pad = pad_rows(value_local, 0)
    gate_pad = pad_rows(gate, 1)
    starts = tile_starts(lengths_row, tile_count)
    tile_ids = jnp.arange(tile_count, dtype=jnp.int32)
    query_tiles = query_local.reshape(tile_count, TILE, full_width)
    grad_tiles = grad_local.reshape(tile_count, TILE, full_width)
    out_tiles = lax.map(lambda task_item: forward_task(task_item[0], task_item[1], task_item[2], key_pad, value_pad, gate_pad, query_gain, head_count), (query_tiles, tile_ids, starts))

    def owner_step(totals, owner_items):
        query_own, grad_own, out_own, id_own = owner_items
        zero_parts = (jnp.zeros(key_pad.shape, jnp.float32), jnp.zeros(value_pad.shape, jnp.float32), jnp.zeros(gate_pad.shape, jnp.float32))

        def task_step(partials, task_item):
            query_tile, grad_tile, out_tile, tile_id = task_item
            return backward_task(partials, query_tile, grad_tile, out_tile, tile_id, starts[tile_id], key_pad, value_pad, gate_pad, query_gain, head_count)
        partials, query_own_grad = lax.scan(task_step, zero_parts, (query_own, grad_own, out_own, id_own))
        key_part, value_part, gate_part = partials
        suffix = jnp.flip(jnp.cumsum(jnp.flip(gate_part[:, :token_count], 1), axis=1), 1)
        rounded = lax.optimization_barrier((key_part[:token_count].astype(jnp.bfloat16), value_part[:token_count].astype(jnp.bfloat16), suffix.astype(jnp.bfloat16)))
        totals = (totals[0] + rounded[0].astype(jnp.float32), totals[1] + rounded[1].astype(jnp.float32), totals[2] + rounded[2].astype(jnp.float32))
        return (totals, query_own_grad)
    zero_totals = (jnp.zeros((token_count, head_dim), jnp.float32), jnp.zeros((token_count, head_dim), jnp.float32), jnp.zeros((head_count, token_count), jnp.float32))
    grouped = (query_tiles.reshape(SERVERS, TILE_DEV, TILE, full_width), grad_tiles.reshape(SERVERS, TILE_DEV, TILE, full_width), out_tiles.reshape(SERVERS, TILE_DEV, TILE, full_width), tile_ids.reshape(SERVERS, TILE_DEV))
    totals, query_grad_tiles = lax.scan(owner_step, zero_totals, grouped)
    normed_key_grad, value_sum, gate_grad = totals
    _, key_pullback = jax.vjp(lambda raw_values, gain_vec: norm_rows(raw_values, gain_vec, 1.0), key_local.astype(jnp.float32), key_gain)
    key_input_grad, key_gain_part = key_pullback(normed_key_grad)
    scale_factor = head_dim ** (-0.5)
    _, query_pullback = jax.vjp(lambda raw_values, gain_vec: norm_rows(raw_values, gain_vec, scale_factor), query_local.reshape(token_count, head_count, head_dim).astype(jnp.float32), query_gain)
    query_input_grad, query_gain_part = query_pullback(query_grad_tiles.reshape(token_count, head_count, head_dim).astype(jnp.float32))
    forget_grad = gate_grad * jax.nn.sigmoid(-logit_local.astype(jnp.float32))
    attention = out_tiles.reshape(token_count, full_width)
    return (attention, query_input_grad.reshape(token_count, full_width).astype(jnp.bfloat16), key_input_grad.astype(jnp.bfloat16), value_sum.astype(jnp.bfloat16), forget_grad, jnp.stack([query_gain_part, key_gain_part]))

def reference(queries, key_vectors, values, forget_logit, out_grad, query_gain, key_gain, lengths):
    results = []
    for replica in range(PACK_TOTAL):
        results.append(one_pack(queries[replica], key_vectors[replica], values[replica], forget_logit[replica], out_grad[replica], query_gain, key_gain, lengths[replica]))
    attention = jnp.stack([entry[0] for entry in results])
    query_grad = jnp.stack([entry[1] for entry in results])
    key_grad = jnp.stack([entry[2] for entry in results])
    value_grad = jnp.stack([entry[3] for entry in results])
    forget_grad = jnp.stack([entry[4] for entry in results])
    norm_gain_grad = results[0][5]
    for replica in range(1, PACK_TOTAL):
        norm_gain_grad = norm_gain_grad + results[replica][5]
    return (attention, query_grad, key_grad, value_grad, forget_grad, norm_gain_grad)
```

```python
import functools
import math

import jax
import jax.numpy as jnp
from jax import lax
from jax.experimental import pallas as pl
from jax.experimental.pallas import tpu as pltpu
from jax.sharding import PartitionSpec as P

MESH = pl.DeviceIdType.MESH
F32 = jnp.float32
BF16 = jnp.bfloat16

EPS = 1e-06
HEADS = 4
DH = 128
TOK = 256
TILE = 64
SHARDS = 32
HEAD_ROWS = 16
ROWS = HEAD_ROWS + TOK
PIECES = ((0, 80), (80, 144), (144, 208), (208, 272))
LOG2E = math.log2(math.e)
LN2 = math.log(2.0)
FAR = (2, -1, 1, 0)


def spot():
    me = lax.axis_index("seq")
    return me // 8, (me // 2) % 4, me % 2


def shard_at(tree, da, db, core=None):
    z, y, c = spot()
    dz, dy = (da, db) if tree == 0 else (db, da)
    c = c if core is None else core
    return (((z + dz + 4) % 4) * 4 + (y + dy + 4) % 4) * 2 + c


def cell_at(tree, da, db):
    z, y, _ = spot()
    dz, dy = (da, db) if tree == 0 else (db, da)
    return ((z + dz + 4) % 4) * 4 + (y + dy + 4) % 4


def piece(tree, part):
    low, high = PIECES[2 * tree], PIECES[2 * tree + 1]
    first, last = {"a": low, "b": high, "ab": (low[0], high[1])}[part]
    return first, last - first


def rows_of(tree, part):
    first, count = piece(tree, part)
    return pl.ds(first, count)


def greet(devices):
    barrier = pltpu.get_barrier_semaphore()
    for device in devices:
        pl.semaphore_signal(barrier, inc=1, device_id=device, device_id_type=MESH)
    pl.semaphore_wait(barrier, len(devices))


def neighbours():
    found = [{"seq": shard_at(tree, step, 0)} for tree in (0, 1) for step in (1, -1)]
    return found + [{"seq": shard_at(0, 0, 0, 1 - spot()[2])}]


def ring_events():
    names = ["A-", "A+", "A2a", "A2b"]
    for da in FAR:
        names += [("B-", da), ("B+", da), ("B2a", da), ("B2b", da)]
    return names


def split3(x):
    high = x.astype(BF16)
    rest = x - high.astype(F32)
    mid = rest.astype(BF16)
    low = (rest - mid.astype(F32)).astype(BF16)
    return high, mid, low


def gather_kernel(key_ref, value_ref, logit_ref, gain_ref, out_ref, mine, send_sem, recv_sem, own_sem):
    greet(neighbours())
    me = lax.axis_index("seq")
    sibling = {"seq": shard_at(0, 0, 0, 1 - spot()[2])}

    raw = key_ref[...].astype(F32)
    scale = lax.rsqrt(jnp.mean(raw * raw, axis=1, keepdims=True) + EPS)
    mine[HEAD_ROWS:, 0:DH] = (raw * scale * gain_ref[...]).astype(BF16)
    mine[HEAD_ROWS:, DH:] = value_ref[...]
    logit = logit_ref[...].astype(F32)
    decay = jnp.minimum(logit, 0.0) - jnp.log1p(jnp.exp(-jnp.abs(logit)))
    row = lax.broadcasted_iota(jnp.int32, (TOK, TOK), 0)
    column = lax.broadcasted_iota(jnp.int32, (TOK, TOK), 1)
    upper = (row <= column).astype(F32)
    local = jnp.dot(decay, upper, preferred_element_type=F32, precision=lax.Precision.HIGHEST)
    high = local.astype(BF16).astype(F32)
    mid = (local - high).astype(BF16).astype(F32)
    low = local - high - mid
    zero = jnp.zeros((4, TOK), F32)
    mine[0:HEAD_ROWS, :] = jnp.concatenate([high, mid, low, zero], axis=0).astype(BF16)

    ids = {}
    for tree in (0, 1):
        for name in ring_events():
            ids[tree, name] = len(ids)
        for da in FAR:
            for db in FAR:
                ids[tree, "D", da, db] = len(ids)
    started = []

    def copy(event, source, place, rows, device):
        number = ids[event]
        made = pltpu.make_async_remote_copy(
            src_ref=source.at[rows],
            dst_ref=out_ref.at[place, rows],
            send_sem=send_sem.at[number],
            recv_sem=recv_sem.at[number],
            device_id=device,
            device_id_type=MESH,
        )
        made.start()
        started.append(made)

    def arrived(event, place, rows):
        number = ids[event]
        part = out_ref.at[place, rows]
        pltpu.make_async_remote_copy(
            src_ref=part,
            dst_ref=part,
            send_sem=send_sem.at[number],
            recv_sem=recv_sem.at[number],
            device_id=sibling,
            device_id_type=MESH,
        ).wait_recv()

    def send(event, tree, da, db, part, target):
        place = shard_at(tree, da, db)
        source = mine if (da, db) == (0, 0) else out_ref.at[place]
        device = {"seq": shard_at(tree, *target)}
        copy(event, source, place, rows_of(tree, part), device)

    def share(tree, da, db):
        place = shard_at(tree, da, db)
        source = mine if (da, db) == (0, 0) else out_ref.at[place]
        copy((tree, "D", da, db), source, place, rows_of(tree, "ab"), sibling)

    def wait(tree, name, da, db, part):
        arrived((tree, name), shard_at(tree, da, db), rows_of(tree, part))

    for tree in (0, 1):
        send((tree, "A-"), tree, 0, 0, "ab", (1, 0))
        send((tree, "A+"), tree, 0, 0, "ab", (-1, 0))
    own = pltpu.make_async_copy(mine, out_ref.at[me], own_sem)
    own.start()
    for tree in (0, 1):
        send((tree, ("B-", 0)), tree, 0, 0, "ab", (0, 1))
        send((tree, ("B+", 0)), tree, 0, 0, "ab", (0, -1))
        share(tree, 0, 0)

    for tree in (0, 1):
        wait(tree, "A-", -1, 0, "ab")
        send((tree, "A2a"), tree, -1, 0, "a", (1, 0))
        wait(tree, "A+", 1, 0, "ab")
        send((tree, "A2b"), tree, 1, 0, "b", (-1, 0))
        for da in (-1, 1):
            send((tree, ("B-", da)), tree, da, 0, "ab", (0, 1))
            send((tree, ("B+", da)), tree, da, 0, "ab", (0, -1))
            share(tree, da, 0)

    def near(tree, da):
        wait(tree, ("B-", da), da, -1, "ab")
        send((tree, ("B2a", da)), tree, da, -1, "a", (0, 1))
        wait(tree, ("B+", da), da, 1, "ab")
        send((tree, ("B2b", da)), tree, da, 1, "b", (0, -1))
        share(tree, da, -1)
        share(tree, da, 1)

    def far(tree, da):
        wait(tree, ("B2a", da), da, 2, "a")
        wait(tree, ("B2b", da), da, 2, "b")
        share(tree, da, 2)

    for tree in (0, 1):
        near(tree, 0)
    for tree in (0, 1):
        wait(tree, "A2a", 2, 0, "a")
        wait(tree, "A2b", 2, 0, "b")
        send((tree, ("B-", 2)), tree, 2, 0, "ab", (0, 1))
        send((tree, ("B+", 2)), tree, 2, 0, "ab", (0, -1))
        share(tree, 2, 0)
    for da in (-1, 1):
        for tree in (0, 1):
            near(tree, da)
    for tree in (0, 1):
        far(tree, 0)
    for tree in (0, 1):
        near(tree, 2)
    for da in (-1, 1, 2):
        for tree in (0, 1):
            far(tree, da)
    other = 1 - spot()[2]
    for tree in (0, 1):
        for da in FAR:
            for db in FAR:
                arrived((tree, "D", da, db), shard_at(tree, da, db, other), rows_of(tree, "ab"))
    for made in started:
        made.wait_send()
    own.wait()


EVENTS = 2 * (20 + 16)


def gather(key_local, value_local, logit_local, key_gain):
    vmem = pl.BlockSpec(memory_space=pltpu.VMEM)
    return pl.pallas_call(
        gather_kernel,
        out_shape=jax.ShapeDtypeStruct((SHARDS, ROWS, 2 * DH), BF16),
        in_specs=[vmem] * 4,
        out_specs=pl.BlockSpec(memory_space=pl.ANY),
        scratch_shapes=[
            pltpu.VMEM((ROWS, 2 * DH), BF16),
            pltpu.SemaphoreType.DMA((EVENTS,)),
            pltpu.SemaphoreType.DMA((EVENTS,)),
            pltpu.SemaphoreType.DMA(()),
        ],
        compiler_params=pltpu.CompilerParams(collective_id=0, has_side_effects=True),
        name="gather_shards",
    )(key_local, value_local, logit_local, key_gain)


def row_to_columns(row):
    parts = [
        jnp.transpose(jnp.broadcast_to(row[:, half * DH : (half + 1) * DH], (DH, DH)))
        for half in (0, 1)
    ]
    return jnp.concatenate(parts, axis=0)


def split_lanes(full):
    high, mid, low = split3(full)
    lane = lax.broadcasted_iota(jnp.int32, full.shape, 1)
    picked = jnp.where(
        lane == 0,
        high.astype(F32),
        jnp.where(lane == 1, mid.astype(F32), jnp.where(lane == 2, low.astype(F32), 0.0)),
    )
    return picked.astype(BF16)


def contract_last(left, right):
    return lax.dot_general(left, right, (((1,), (1,)), ((), ())), preferred_element_type=F32)


def contract_first(left, right):
    return lax.dot_general(left, right, (((0,), (0,)), ((), ())), preferred_element_type=F32)


def attend_kernel(
    place_ref,
    length_ref,
    kv_ref,
    query_ref,
    grad_ref,
    query_gain_ref,
    key_gain_ref,
    att_ref,
    query_grad_ref,
    part_ref,
    gain_ref,
    gate,
    query_wide,
    query_low,
    grad_wide,
    grad_low,
    prob,
    score_low,
    out_sum,
    column,
    key_gain_sum,
):
    me = place_ref[0]
    ones = jnp.ones((TOK, DH), BF16)

    starts = []
    for tile in range(TOK // TILE):
        at = me * (TOK // TILE) + tile
        end = jnp.int32(0)
        start = jnp.int32(0)
        for document in range(4):
            end = end + length_ref[document]
            start = jnp.where(end <= at, end, start)
        starts.append(start * TILE)
    low_block = starts[0] // TOK

    carry = jnp.zeros((4, DH), F32)
    for shard in range(SHARDS):
        packed = kv_ref[shard, 0:HEAD_ROWS, :].astype(F32)
        local = (packed[0:4] + packed[4:8] + packed[8:12]) * LOG2E
        gate[shard, 0:4, :] = local + jnp.concatenate([carry, carry], axis=1)
        carry = carry + jnp.broadcast_to(local[:, TOK - 1 :], (4, DH))

    query_scale = query_gain_ref[...] * (DH**-0.5)
    for head in range(HEADS):
        raw = query_ref[:, head * DH : (head + 1) * DH].astype(F32)
        scale = lax.rsqrt(jnp.mean(raw * raw, axis=1, keepdims=True) + EPS)
        normed = (raw * scale * (query_scale * LOG2E)).astype(BF16)
        own_gate = row_to_columns(gate[me, head : head + 1, :])
        query_low[head * TOK : (head + 1) * TOK, :] = normed
        query_wide[head] = jnp.concatenate([normed, split_lanes(own_gate)], axis=1)
    out_sum[...] = jnp.zeros_like(out_sum)
    column[...] = jnp.zeros_like(column)
    key_gain_sum[...] = jnp.zeros_like(key_gain_sum)

    lane_token = lax.broadcasted_iota(jnp.int32, (1, TOK), 1)

    def forward_block(block, diagonal):
        keys = kv_ref[block, HEAD_ROWS:, 0:DH]
        values = kv_ref[block, HEAD_ROWS:, DH:]
        key_wide = jnp.concatenate([keys, ones], axis=1)
        value_wide = jnp.concatenate([values, ones], axis=1)
        token = block * TOK + lane_token
        for head in range(HEADS):
            scores = contract_last(query_wide[head], key_wide)
            key_gate = gate[block, head : head + 1, :]
            pieces = []
            for tile in range(TOK // TILE):
                low = jnp.where(token >= starts[tile], key_gate, jnp.inf)
                pieces.append(scores[tile * TILE : (tile + 1) * TILE] - low)
            scores = jnp.concatenate(pieces, axis=0)
            if diagonal:
                row = lax.broadcasted_iota(jnp.int32, (TOK, TOK), 0)
                col = lax.broadcasted_iota(jnp.int32, (TOK, TOK), 1)
                scores = jnp.where(col <= row, scores, -jnp.inf)
            weights = jnp.exp2(scores).astype(BF16)
            prob[block, head * TOK : (head + 1) * TOK, :] = weights
            out_sum[head] += jnp.dot(weights, value_wide, preferred_element_type=F32)

    def forward_step(block, _):
        forward_block(block, False)
        return 0

    lax.fori_loop(low_block, me, forward_step, 0)
    forward_block(me, True)

    for head in range(HEADS):
        span = slice(head * DH, (head + 1) * DH)
        inverse = 1.0 / out_sum[head, :, DH:]
        out = out_sum[head, :, 0:DH] * inverse
        att_ref[:, span] = out.astype(BF16)
        scaled = (grad_ref[:, span].astype(F32) * inverse).astype(BF16)
        inner = jnp.sum(scaled.astype(F32) * out, axis=1, keepdims=True)
        grad_low[head * TOK : (head + 1) * TOK, :] = scaled
        grad_wide[head] = jnp.concatenate(
            [scaled, split_lanes(jnp.broadcast_to(-inner, (TOK, DH)))], axis=1
        )
    out_sum[...] = jnp.zeros_like(out_sum)

    def clear_step(block, _):
        part_ref[block] = jnp.zeros((ROWS, 2 * DH), BF16)
        return 0

    lax.fori_loop(0, low_block, clear_step, 0)
    lax.fori_loop(me + 1, SHARDS, clear_step, 0)

    def backward_step(block, _):
        keys = kv_ref[block, HEAD_ROWS:, 0:DH]
        values = kv_ref[block, HEAD_ROWS:, DH:]
        key_wide = jnp.concatenate([keys, ones], axis=1)
        value_wide = jnp.concatenate([values, ones], axis=1)
        for head in range(HEADS):
            span = slice(head * TOK, (head + 1) * TOK)
            prob_grad = contract_last(grad_wide[head], value_wide)
            score_grad = prob[block, span, :].astype(F32) * prob_grad
            low = score_grad.astype(BF16)
            folded = jnp.sum(low.astype(F32).reshape(TOK // 8, 8, TOK), axis=0)
            column[block, head : head + 1, :] = -jnp.sum(folded, axis=0, keepdims=True)
            score_low[span, :] = low
            out_sum[head] += jnp.dot(low, key_wide, preferred_element_type=F32)
        key_part = contract_first(score_low[...], query_low[...]) * LN2
        value_part = contract_first(prob[block], grad_low[...])
        part_ref[block, HEAD_ROWS:, 0:DH] = key_part.astype(BF16)
        part_ref[block, HEAD_ROWS:, DH:] = value_part.astype(BF16)
        moved = (key_part * keys.astype(F32)).reshape(TOK // 8, 8, DH)
        key_gain_sum[...] += jnp.sum(moved, axis=0)
        return 0

    lax.fori_loop(low_block, me + 1, backward_step, 0)

    query_gain_sum = jnp.zeros((1, DH), F32)
    for head in range(HEADS):
        span = slice(head * DH, (head + 1) * DH)
        raw = query_ref[:, span].astype(F32)
        scale = lax.rsqrt(jnp.mean(raw * raw, axis=1, keepdims=True) + EPS)
        hat = raw * scale
        cotangent = out_sum[head, :, 0:DH]
        query_gain_sum += jnp.sum(cotangent * hat, axis=0, keepdims=True)
        inner = cotangent * query_scale
        mean = jnp.mean(inner * hat, axis=1, keepdims=True)
        query_grad_ref[:, span] = (scale * (inner - hat * mean)).astype(BF16)
        for half in (0, 1):
            tokens = slice(half * DH, (half + 1) * DH)
            turned = jnp.transpose(out_sum[head, tokens, DH:])
            column[me, head : head + 1, tokens] += turned[0:1]
    query_gain_sum = query_gain_sum * (DH**-0.5)
    key_gain_row = jnp.sum(key_gain_sum[...], axis=0, keepdims=True) / key_gain_ref[...]
    gain_ref[...] = jnp.concatenate([query_gain_sum, key_gain_row, jnp.zeros((6, DH), F32)], axis=0)

    carry = jnp.zeros((8, 1), F32)
    last = lax.broadcasted_iota(jnp.int32, (8, TOK), 1) == TOK - 1
    for shard in range(SHARDS - 1, -1, -1):
        local = column[shard]
        whole = local + jnp.where(last, jnp.broadcast_to(carry, (8, TOK)), 0.0)
        high = whole.astype(BF16).astype(F32)
        part_ref[shard, 0:HEAD_ROWS, :] = jnp.concatenate([high, whole - high], axis=0).astype(BF16)
        carry = carry + jnp.sum(local, axis=1, keepdims=True)


def attend(place, lengths_row, shards, query_local, grad_local, query_gain, key_gain):
    vmem = pl.BlockSpec(memory_space=pltpu.VMEM)
    smem = pl.BlockSpec(memory_space=pltpu.SMEM)
    wide = jax.ShapeDtypeStruct((TOK, HEADS * DH), BF16)
    rows = HEADS * TOK
    return pl.pallas_call(
        attend_kernel,
        out_shape=(
            wide,
            wide,
            jax.ShapeDtypeStruct((SHARDS, ROWS, 2 * DH), BF16),
            jax.ShapeDtypeStruct((8, DH), F32),
        ),
        in_specs=[smem, smem] + [vmem] * 5,
        out_specs=(vmem,) * 4,
        scratch_shapes=[
            pltpu.VMEM((SHARDS, 8, TOK), F32),
            pltpu.VMEM((HEADS, TOK, 2 * DH), BF16),
            pltpu.VMEM((rows, DH), BF16),
            pltpu.VMEM((HEADS, TOK, 2 * DH), BF16),
            pltpu.VMEM((rows, DH), BF16),
            pltpu.VMEM((SHARDS, rows, TOK), BF16),
            pltpu.VMEM((rows, TOK), BF16),
            pltpu.VMEM((HEADS, TOK, 2 * DH), F32),
            pltpu.VMEM((SHARDS, 8, TOK), F32),
            pltpu.VMEM((8, DH), F32),
        ],
        compiler_params=pltpu.CompilerParams(vmem_limit_bytes=56 * 2**20),
        name="attend_both",
    )(place, lengths_row, shards, query_local, grad_local, query_gain, key_gain)


def scatter_kernel(
    part_ref,
    gain_ref,
    key_ref,
    logit_ref,
    key_gain_ref,
    key_grad_ref,
    value_grad_ref,
    forget_grad_ref,
    gain_out_ref,
    twin,
    total,
    landed,
    gain_sum,
    gain_landed,
    send_sem,
    recv_sem,
    gain_send,
    gain_recv,
):
    z, y, core = spot()
    rep = lax.axis_index("rep")
    sibling = {"seq": shard_at(0, 0, 0, 1 - core)}
    partners = []
    partners.append([{"rep": (rep + step) % 4} for step in (1, 2, 3)])
    partners.append([{"seq": shard_at(0, step, 0)} for step in (1, 2, 3)])
    partners.append([{"seq": shard_at(1, step, 0)} for step in (1, 2, 3)])
    partners.append([sibling])
    greet([device for group in partners for device in group])

    ids = {}
    for tree in (0, 1):
        for name in ring_events():
            ids[tree, name] = len(ids)
    slot = dict(ids)
    for tree in (0, 1):
        for da in FAR:
            for db in FAR:
                ids[tree, "D", da, db] = len(ids)
    started = []

    def copy(number, source, target, device):
        made = pltpu.make_async_remote_copy(
            src_ref=source,
            dst_ref=target,
            send_sem=send_sem.at[number],
            recv_sem=recv_sem.at[number],
            device_id=device,
            device_id_type=MESH,
        )
        made.start()
        started.append(made)

    def arrived(number, target):
        pltpu.make_async_remote_copy(
            src_ref=target,
            dst_ref=target,
            send_sem=send_sem.at[number],
            recv_sem=recv_sem.at[number],
            device_id=sibling,
            device_id_type=MESH,
        ).wait_recv()

    def land(tree, name, part):
        first, count = piece(tree, part)
        return landed.at[slot[tree, name], pl.ds(first - piece(tree, "ab")[0], count)]

    def send(event, tree, da, db, part, target):
        source = total.at[cell_at(tree, da, db), rows_of(tree, part)]
        copy(ids[event], source, land(event[0], event[1], part), {"seq": shard_at(tree, *target)})

    def added(tree, part, terms):
        lifted = [term.astype(F32) for term in terms]
        return functools.reduce(lambda a, b: a + b, lifted)

    def store(target, tree, part, whole):
        if tree == 0 and part in ("a", "ab"):
            gates = whole[0:8] + whole[8:16]
            high = gates.astype(BF16).astype(F32)
            whole = jnp.concatenate([high, gates - high, whole[16:]], axis=0)
        target[...] = whole.astype(BF16)

    def wait_twin(tree, da, db, part="ab"):
        place = cell_at(tree, da, db)
        arrived(ids[tree, "D", da, db], twin.at[place, rows_of(tree, "ab")])

    def twins(tree, da, db, part):
        place, rows = cell_at(tree, da, db), rows_of(tree, part)
        return [part_ref[shard_at(tree, da, db), rows, :], twin[place, rows, :]]

    def put(tree, da, db, part, terms):
        store(total.at[cell_at(tree, da, db), rows_of(tree, part)], tree, part, added(tree, part, terms))

    def gain_copies(axis):
        first = 3 * axis
        return [
            pltpu.make_async_remote_copy(
                src_ref=gain_sum.at[axis],
                dst_ref=gain_landed.at[first + i],
                send_sem=gain_send.at[first + i],
                recv_sem=gain_recv.at[first + i],
                device_id=device,
                device_id_type=MESH,
            )
            for i, device in enumerate(partners[axis])
        ]

    def gain_start(axis):
        for made in gain_copies(axis):
            made.start()

    def gain_add(axis):
        whole = gain_sum[axis]
        for i, made in enumerate(gain_copies(axis)):
            made.wait_recv()
            whole = whole + gain_landed[3 * axis + i]
        for made in gain_copies(axis):
            made.wait_send()
        gain_sum[axis + 1] = whole

    gain_sum[0] = gain_ref[...]
    order = [(da, 2) for da in FAR] + [(da, db) for da in FAR for db in (1, -1)] + [(da, 0) for da in FAR]
    for da, db in order:
        for tree in (0, 1):
            rows = rows_of(tree, "ab")
            source = part_ref.at[shard_at(tree, da, db, 1 - core), rows]
            copy(ids[tree, "D", da, db], source, twin.at[cell_at(tree, da, db), rows], sibling)
    gain_start(0)

    for da in FAR:
        for tree in (0, 1):
            wait_twin(tree, da, 2)
            put(tree, da, 2, "ab", twins(tree, da, 2, "ab"))
            send((tree, ("B2a", da)), tree, da, 2, "a", (0, 1))
            send((tree, ("B2b", da)), tree, da, 2, "b", (0, -1))
    gain_add(0)
    gain_start(1)
    for da in FAR:
        for tree in (0, 1):
            for db, name, near, far in ((1, "B2a", "a", "b"), (-1, "B2b", "b", "a")):
                wait_twin(tree, da, db)
                put(tree, da, db, far, twins(tree, da, db, far))
                target = land(tree, (name, da), near)
                arrived(ids[tree, (name, da)], target)
                put(tree, da, db, near, twins(tree, da, db, near) + [target[...]])
                send((tree, ("B-" if db == 1 else "B+", da)), tree, da, db, "ab", (0, db))
    gain_add(1)
    gain_start(2)
    finals = []
    for da in FAR:
        for tree in (0, 1):
            wait_twin(tree, da, 0)
            terms = twins(tree, da, 0, "ab")
            for name in ("B-", "B+"):
                target = land(tree, (name, da), "ab")
                arrived(ids[tree, (name, da)], target)
                terms.append(target[...])
            put(tree, da, 0, "ab", terms)
            here = total.at[cell_at(tree, da, 0)]
            if da == 2:
                send((tree, "A2a"), tree, 2, 0, "a", (1, 0))
                send((tree, "A2b"), tree, 2, 0, "b", (-1, 0))
            if da in (-1, 1):
                name, part = ("A2a", "a") if da == 1 else ("A2b", "b")
                target = land(tree, name, part)
                arrived(ids[tree, name], target)
                rows = rows_of(tree, part)
                put(tree, da, 0, part, [here[rows, :], target[...]])
                send((tree, "A-" if da == 1 else "A+"), tree, da, 0, "ab", (da, 0))
    gain_add(2)
    gain_start(3)
    for tree in (0, 1):
        terms = [total[cell_at(tree, 0, 0), rows_of(tree, "ab"), :]]
        for name in ("A-", "A+"):
            target = land(tree, name, "ab")
            arrived(ids[tree, name], target)
            terms.append(target[...])
        finals.append(added(tree, "ab", terms))
    gain_add(3)

    whole = jnp.concatenate([finals[0][HEAD_ROWS:], finals[1]], axis=0)
    value_grad_ref[...] = whole[:, DH:].astype(BF16)
    cotangent = whole[:, 0:DH]
    raw = key_ref[...].astype(F32)
    scale = lax.rsqrt(jnp.mean(raw * raw, axis=1, keepdims=True) + EPS)
    hat = raw * scale
    inner = cotangent * key_gain_ref[...]
    mean = jnp.mean(inner * hat, axis=1, keepdims=True)
    key_grad_ref[...] = (scale * (inner - hat * mean)).astype(BF16)

    gates = finals[0][0:4] + finals[0][8:12]
    row = lax.broadcasted_iota(jnp.int32, (TOK, TOK), 0)
    col = lax.broadcasted_iota(jnp.int32, (TOK, TOK), 1)
    lower = (row >= col).astype(F32)
    suffix = jnp.dot(gates, lower, preferred_element_type=F32, precision=lax.Precision.HIGHEST)
    logit = logit_ref[...].astype(F32)
    forget_grad_ref[...] = suffix / (1.0 + jnp.exp(logit))
    gain_out_ref[...] = gain_sum[4][0:2]
    for made in started:
        made.wait_send()


def scatter(parts, gains, key_local, logit_local, key_gain):
    vmem = pl.BlockSpec(memory_space=pltpu.VMEM)
    rows = jax.ShapeDtypeStruct((TOK, DH), BF16)
    return pl.pallas_call(
        scatter_kernel,
        out_shape=(
            rows,
            rows,
            jax.ShapeDtypeStruct((HEADS, TOK), F32),
            jax.ShapeDtypeStruct((2, DH), F32),
        ),
        in_specs=[vmem] * 5,
        out_specs=(vmem,) * 4,
        scratch_shapes=[
            pltpu.VMEM((SHARDS // 2, ROWS, 2 * DH), BF16),
            pltpu.VMEM((SHARDS // 2, ROWS, 2 * DH), BF16),
            pltpu.VMEM((40, PIECES[1][1], 2 * DH), BF16),
            pltpu.VMEM((5, 8, DH), F32),
            pltpu.VMEM((10, 8, DH), F32),
            pltpu.SemaphoreType.DMA((EVENTS,)),
            pltpu.SemaphoreType.DMA((EVENTS,)),
            pltpu.SemaphoreType.DMA((10,)),
            pltpu.SemaphoreType.DMA((10,)),
        ],
        compiler_params=pltpu.CompilerParams(
            collective_id=1, has_side_effects=True, vmem_limit_bytes=40 * 2**20
        ),
        name="scatter_sums",
    )(parts, gains, key_local, logit_local, key_gain)


def on_device(queries, key_vectors, values, forget_logit, out_grad, query_gain, key_gain, lengths):
    key_gain = key_gain.reshape(1, DH)
    query_gain = query_gain.reshape(1, DH)
    key_local, logit_local = key_vectors[0], forget_logit[0]
    place = lax.axis_index("seq").astype(jnp.int32).reshape(1)
    shards = gather(key_local, values[0], logit_local, key_gain)
    attention, query_grad, parts, gains = attend(
        place, lengths[0], shards, queries[0], out_grad[0], query_gain, key_gain
    )
    key_grad, value_grad, forget_grad, gain_grad = scatter(
        parts, gains, key_local, logit_local, key_gain
    )
    return (
        attention[None],
        query_grad[None],
        key_grad[None],
        value_grad[None],
        forget_grad[None],
        gain_grad,
    )


def solution(mesh):
    return jax.shard_map(
        on_device,
        mesh=mesh,
        in_specs=(
            P("rep", "seq", None),
            P("rep", "seq", None),
            P("rep", "seq", None),
            P("rep", None, "seq"),
            P("rep", "seq", None),
            P(),
            P(),
            P("rep", None),
        ),
        out_specs=(
            P("rep", "seq", None),
            P("rep", "seq", None),
            P("rep", "seq", None),
            P("rep", "seq", None),
            P("rep", None, "seq"),
            P(),
        ),
        check_vma=False,
    )
```

```python
import functools
import math

import jax
import jax.numpy as jnp
from jax import lax
from jax.experimental import pallas as pl
from jax.experimental.pallas import tpu as pltpu
from jax.sharding import PartitionSpec as P

MESH = pl.DeviceIdType.MESH
F32 = jnp.float32
BF16 = jnp.bfloat16

EPS = 1e-06
HEADS = 4
DH = 128
TOK = 256
TILE = 64
SHARDS = 32
HEAD_ROWS = 16
ROWS = HEAD_ROWS + TOK
PIECES = ((0, 80), (80, 144), (144, 208), (208, 272))
LOG2E = math.log2(math.e)
LN2 = math.log(2.0)
FAR = (2, -1, 1, 0)
BACK = 24
ORDER = (
    (0, 0), (-1, 0), (0, -1), (1, 0), (0, 1), (-1, -1), (-1, 1), (1, -1),
    (1, 1), (2, 0), (0, 2), (2, -1), (-1, 2), (2, 1), (1, 2), (2, 2),
)
STEPS = len(ORDER)


def spot():
    me = lax.axis_index("seq")
    return me // 8, (me // 2) % 4, me % 2


def shard_at(tree, da, db, core=None):
    z, y, c = spot()
    dz, dy = (da, db) if tree == 0 else (db, da)
    c = c if core is None else core
    return (((z + dz + 4) % 4) * 4 + (y + dy + 4) % 4) * 2 + c


def cell_at(tree, da, db):
    z, y, _ = spot()
    dz, dy = (da, db) if tree == 0 else (db, da)
    return ((z + dz + 4) % 4) * 4 + (y + dy + 4) % 4


def piece(tree, part):
    low, high = PIECES[2 * tree], PIECES[2 * tree + 1]
    first, last = {"a": low, "b": high, "ab": (low[0], high[1])}[part]
    return first, last - first


def rows_of(tree, part):
    first, count = piece(tree, part)
    return pl.ds(first, count)


def greet(devices):
    barrier = pltpu.get_barrier_semaphore()
    for device in devices:
        pl.semaphore_signal(barrier, inc=1, device_id=device, device_id_type=MESH)
    pl.semaphore_wait(barrier, len(devices))


def ring_events():
    names = ["A-", "A+", "A2a", "A2b"]
    for da in FAR:
        names += [("B-", da), ("B+", da), ("B2a", da), ("B2b", da)]
    return names


def split3(x):
    high = x.astype(BF16)
    rest = x - high.astype(F32)
    mid = rest.astype(BF16)
    low = (rest - mid.astype(F32)).astype(BF16)
    return high, mid, low


def row_to_columns(row):
    parts = [
        jnp.transpose(jnp.broadcast_to(row[:, half * DH : (half + 1) * DH], (DH, DH)))
        for half in (0, 1)
    ]
    return jnp.concatenate(parts, axis=0)


def split_lanes(full):
    high, mid, low = split3(full)
    lane = lax.broadcasted_iota(jnp.int32, full.shape, 1)
    picked = jnp.where(
        lane == 0,
        high.astype(F32),
        jnp.where(lane == 1, mid.astype(F32), jnp.where(lane == 2, low.astype(F32), 0.0)),
    )
    return picked.astype(BF16)


def contract_last(left, right):
    return lax.dot_general(left, right, (((1,), (1,)), ((), ())), preferred_element_type=F32)


def contract_first(left, right):
    return lax.dot_general(left, right, (((0,), (0,)), ((), ())), preferred_element_type=F32)


def pick(step, entries):
    found = jnp.int32(entries[0])
    for i, entry in enumerate(entries):
        if i:
            found = jnp.where(step == i, jnp.int32(entry), found)
    return found


def step_of(tree, da, db):
    return ORDER.index((da, db) if tree == 0 else (db, da))


def fused_kernel(
    length_ref,
    key_ref,
    value_ref,
    logit_ref,
    query_ref,
    grad_ref,
    query_gain_ref,
    key_gain_ref,
    att_ref,
    query_grad_ref,
    key_grad_ref,
    value_grad_ref,
    forget_grad_ref,
    gain_out_ref,
    shards,
    chunk_sum,
    base,
    query_wide,
    query_low,
    grad_wide,
    grad_low,
    prob,
    score_low,
    out_sum,
    key_gain_sum,
    offset,
    parts,
    twin,
    total,
    landed,
    small,
    small_landed,
    out_send,
    out_recv,
    back_send,
    back_recv,
    sum_send,
    sum_recv,
    small_send,
    small_recv,
):
    me = lax.axis_index("seq")
    z, y, core = spot()
    rep = lax.axis_index("rep")
    sibling = {"seq": shard_at(0, 0, 0, 1 - core)}
    partners = [[sibling]]
    partners.append([{"seq": shard_at(0, step, 0)} for step in (1, 2, 3)])
    partners.append([{"seq": shard_at(1, step, 0)} for step in (1, 2, 3)])
    partners.append([{"rep": (rep + step) % 4} for step in (1, 2, 3)])
    greet([device for group in partners for device in group])

    def remote(source, target, sends, receives, number, device):
        return pltpu.make_async_remote_copy(
            src_ref=source,
            dst_ref=target,
            send_sem=sends.at[number],
            recv_sem=receives.at[number],
            device_id=device,
            device_id_type=MESH,
        )


    raw = key_ref[...].astype(F32)
    scale = lax.rsqrt(jnp.mean(raw * raw, axis=1, keepdims=True) + EPS)
    shards[me, HEAD_ROWS:, 0:DH] = (raw * scale * key_gain_ref[...]).astype(BF16)
    shards[me, HEAD_ROWS:, DH:] = value_ref[...]
    logit = logit_ref[...].astype(F32)
    decay = jnp.minimum(logit, 0.0) - jnp.log1p(jnp.exp(-jnp.abs(logit)))
    row = lax.broadcasted_iota(jnp.int32, (TOK, TOK), 0)
    col = lax.broadcasted_iota(jnp.int32, (TOK, TOK), 1)
    upper = (row <= col).astype(F32)
    local = jnp.dot(decay, upper, preferred_element_type=F32, precision=lax.Precision.HIGHEST)
    local = local * LOG2E
    high = local.astype(BF16).astype(F32)
    mid = (local - high).astype(BF16).astype(F32)
    packed = [high, mid, local - high - mid, jnp.zeros((4, TOK), F32)]
    shards[me, 0:HEAD_ROWS, :] = jnp.concatenate(packed, axis=0).astype(BF16)

    ids = {}
    for tree in (0, 1):
        for name in ring_events():
            ids[tree, name] = len(ids)
    rings = len(ids)


    sent = []

    def send(event, tree, da, db, part, target):
        place = shards.at[shard_at(tree, da, db), rows_of(tree, part)]
        device = {"seq": shard_at(tree, *target)}
        remote(place, place, out_send, out_recv, ids[event], device).start()
        sent.append((ids[event], tree, part))

    def share(tree, da, db):
        place = shards.at[shard_at(tree, da, db), rows_of(tree, "ab")]
        number = rings + 2 * step_of(tree, da, db) + tree
        remote(place, place, out_send, out_recv, number, sibling).start()
        sent.append((number, tree, "ab"))

    def wait(tree, name, da, db, part):
        place = shards.at[shard_at(tree, da, db), rows_of(tree, part)]
        remote(place, place, out_send, out_recv, ids[tree, name], sibling).wait_recv()

    for tree in (0, 1):
        send((tree, "A-"), tree, 0, 0, "ab", (1, 0))
        send((tree, "A+"), tree, 0, 0, "ab", (-1, 0))

    chunk_sum[core, y, z] = jnp.concatenate(
        [jnp.broadcast_to(local[:, TOK - 1 :], (4, DH)), jnp.zeros((4, DH), F32)], axis=0
    )

    def sum_copies(axis):
        if axis == 0:
            place = chunk_sum.at[core, y, z]
        elif axis == 1:
            place = chunk_sum.at[core, y]
        else:
            place = chunk_sum.at[core]
        devices = partners[axis + 1] if axis < 2 else partners[0]
        return [
            remote(place, place, sum_send, sum_recv, 3 * axis + i, device)
            for i, device in enumerate(devices)
        ]

    def sum_wait(axis):
        for i in range(3 if axis < 2 else 1):
            if axis == 0:
                place = chunk_sum.at[core, y, (z + 3 - i) % 4]
            elif axis == 1:
                place = chunk_sum.at[core, (y + 3 - i) % 4]
            else:
                place = chunk_sum.at[1 - core]
            remote(place, place, sum_send, sum_recv, 3 * axis + i, sibling).wait_recv()

    for made in sum_copies(0):
        made.start()
    for tree in (0, 1):
        send((tree, ("B-", 0)), tree, 0, 0, "ab", (0, 1))
        send((tree, ("B+", 0)), tree, 0, 0, "ab", (0, -1))
        share(tree, 0, 0)

    def axis_near():
        for tree in (0, 1):
            wait(tree, "A-", -1, 0, "ab")
            send((tree, "A2a"), tree, -1, 0, "a", (1, 0))
            wait(tree, "A+", 1, 0, "ab")
            send((tree, "A2b"), tree, 1, 0, "b", (-1, 0))
            for da in (-1, 1):
                send((tree, ("B-", da)), tree, da, 0, "ab", (0, 1))
                send((tree, ("B+", da)), tree, da, 0, "ab", (0, -1))
                share(tree, da, 0)

    def axis_far():
        for tree in (0, 1):
            wait(tree, "A2a", 2, 0, "a")
            wait(tree, "A2b", 2, 0, "b")
            send((tree, ("B-", 2)), tree, 2, 0, "ab", (0, 1))
            send((tree, ("B+", 2)), tree, 2, 0, "ab", (0, -1))
            share(tree, 2, 0)

    def near(da):
        for tree in (0, 1):
            wait(tree, ("B-", da), da, -1, "ab")
            send((tree, ("B2a", da)), tree, da, -1, "a", (0, 1))
            wait(tree, ("B+", da), da, 1, "ab")
            send((tree, ("B2b", da)), tree, da, 1, "b", (0, -1))
            share(tree, da, -1)
            share(tree, da, 1)

    def far(da):
        for tree in (0, 1):
            wait(tree, ("B2a", da), da, 2, "a")
            wait(tree, ("B2b", da), da, 2, "b")
            share(tree, da, 2)

    gather_steps = {
        0: [axis_near],
        1: [functools.partial(near, 0)],
        2: [axis_far],
        3: [functools.partial(near, -1)],
        4: [functools.partial(near, 1)],
        5: [functools.partial(far, 0)],
        6: [functools.partial(near, 2)],
        7: [functools.partial(far, -1)],
        8: [functools.partial(far, 1)],
        9: [functools.partial(far, 2)],
    }


    ones = jnp.ones((TOK, DH), BF16)
    starts = []
    for tile in range(TOK // TILE):
        at = me * (TOK // TILE) + tile
        end = jnp.int32(0)
        start = jnp.int32(0)
        for document in range(4):
            end = end + length_ref[document]
            start = jnp.where(end <= at, end, start)
        starts.append(start * TILE)
    query_scale = query_gain_ref[...] * (DH**-0.5)
    for head in range(HEADS):
        raw = query_ref[:, head * DH : (head + 1) * DH].astype(F32)
        scale = lax.rsqrt(jnp.mean(raw * raw, axis=1, keepdims=True) + EPS)
        normed = (raw * scale * (query_scale * LOG2E)).astype(BF16)
        own_gate = row_to_columns(local[head : head + 1, :])
        query_low[head * TOK : (head + 1) * TOK, :] = normed
        query_wide[head] = jnp.concatenate([normed, split_lanes(own_gate)], axis=1)
    out_sum[...] = jnp.zeros_like(out_sum)
    key_gain_sum[...] = jnp.zeros_like(key_gain_sum)
    offset[...] = jnp.zeros_like(offset)
    lane_token = lax.broadcasted_iota(jnp.int32, (1, TOK), 1)

    def forward_block(block, diagonal):
        keys = shards[block, HEAD_ROWS:, 0:DH]
        values = shards[block, HEAD_ROWS:, DH:]
        key_wide = jnp.concatenate([keys, ones], axis=1)
        value_wide = jnp.concatenate([values, ones], axis=1)
        token = block * TOK + lane_token
        packed = shards[block, 0:HEAD_ROWS, :].astype(F32)
        gate = packed[0:4] + packed[4:8] + packed[8:12]
        if not diagonal:
            before = base[block, 0:4, :]
            gate = gate + jnp.concatenate([before, before], axis=1)
        for head in range(HEADS):
            scores = contract_last(query_wide[head], key_wide)
            pieces = []
            for tile in range(TOK // TILE):
                low = jnp.where(token >= starts[tile], gate[head : head + 1], jnp.inf)
                pieces.append(scores[tile * TILE : (tile + 1) * TILE] - low)
            scores = jnp.concatenate(pieces, axis=0)
            if diagonal:
                row = lax.broadcasted_iota(jnp.int32, (TOK, TOK), 0)
                col = lax.broadcasted_iota(jnp.int32, (TOK, TOK), 1)
                scores = jnp.where(col <= row, scores, -jnp.inf)
            weights = jnp.exp2(scores).astype(BF16)
            prob[me - block, head * TOK : (head + 1) * TOK, :] = weights
            out_sum[head] += jnp.dot(weights, value_wide, preferred_element_type=F32)

    sum_wait(0)
    for made in sum_copies(1):
        made.start()
    forward_block(me, True)
    sum_wait(1)
    for made in sum_copies(2):
        made.start()
    sum_wait(2)

    carry = jnp.zeros((8, DH), F32)
    for shard in range(SHARDS - 1, -1, -1):
        chunk = chunk_sum[shard % 2, (shard // 2) % 4, shard // 8]
        carry = carry - jnp.where(shard < me, chunk, 0.0)
        base[shard] = carry

    def chip_of(step):
        dz = pick(step, [entry[0] for entry in ORDER])
        dy = pick(step, [entry[1] for entry in ORDER])
        return cell_at(0, dz, dy)

    def forward_step(step, _):
        for at, actions in gather_steps.items():

            @pl.when(step == at)
            def _():
                for action in actions:
                    action()

        cell = chip_of(step)

        def one(which, _):
            block = cell * 2 + jnp.where(which == 0, core, 1 - core)

            @pl.when(which == 1)
            def _():
                for tree in (0, 1):
                    place = shards.at[block, rows_of(tree, "ab")]
                    number = rings + 2 * step + tree
                    remote(place, place, out_send, out_recv, number, sibling).wait_recv()

            @pl.when((block < me) & (block >= me - BACK))
            def _():
                forward_block(block, False)

            return 0

        return lax.fori_loop(0, 2, one, 0)

    lax.fori_loop(0, STEPS, forward_step, 0)

    for head in range(HEADS):
        span = slice(head * DH, (head + 1) * DH)
        inverse = 1.0 / out_sum[head, :, DH:]
        out = out_sum[head, :, 0:DH] * inverse
        att_ref[:, span] = out.astype(BF16)
        scaled = (grad_ref[:, span].astype(F32) * inverse).astype(BF16)
        inner = jnp.sum(scaled.astype(F32) * out, axis=1, keepdims=True)
        grad_low[head * TOK : (head + 1) * TOK, :] = scaled
        grad_wide[head] = jnp.concatenate(
            [scaled, split_lanes(jnp.broadcast_to(-inner, (TOK, DH)))], axis=1
        )
    out_sum[...] = jnp.zeros_like(out_sum)


    back = []

    def land(tree, name, part):
        first, count = piece(tree, part)
        return landed.at[ids[tree, name], pl.ds(first - piece(tree, "ab")[0], count)]

    def give(event, tree, da, db, part, target):
        source = total.at[cell_at(tree, da, db), rows_of(tree, part)]
        device = {"seq": shard_at(tree, *target)}
        goal = land(event[0], event[1], part)
        remote(source, goal, back_send, back_recv, ids[event], device).start()
        back.append((ids[event], event[0], event[1], part))

    def landing(tree, name, part):
        goal = land(tree, name, part)
        remote(goal, goal, back_send, back_recv, ids[tree, name], sibling).wait_recv()
        return goal[...]

    def added(terms):
        return functools.reduce(lambda a, b: a + b, [term.astype(F32) for term in terms])

    def put(tree, da, db, part, terms):
        whole = added(terms)
        if tree == 0 and part in ("a", "ab"):
            gates = whole[0:8] + whole[8:16]
            high = gates.astype(BF16).astype(F32)
            whole = jnp.concatenate([high, gates - high, whole[16:]], axis=0)
        total[cell_at(tree, da, db), rows_of(tree, part), :] = whole.astype(BF16)

    def twins(tree, da, db, part):
        place, rows = cell_at(tree, da, db), rows_of(tree, part)
        return [parts[shard_at(tree, da, db), rows, :], twin[place, rows, :]]

    def reduce_item(tree, da, db):
        if db == 2:
            put(tree, da, 2, "ab", twins(tree, da, 2, "ab"))
            give((tree, ("B2a", da)), tree, da, 2, "a", (0, 1))
            give((tree, ("B2b", da)), tree, da, 2, "b", (0, -1))
        elif db in (1, -1):
            name, close, away = ("B2a", "a", "b") if db == 1 else ("B2b", "b", "a")
            put(tree, da, db, away, twins(tree, da, db, away))
            put(tree, da, db, close, twins(tree, da, db, close) + [landing(tree, (name, da), close)])
            give((tree, ("B-" if db == 1 else "B+", da)), tree, da, db, "ab", (0, db))
        else:
            terms = twins(tree, da, 0, "ab")
            terms += [landing(tree, (name, da), "ab") for name in ("B-", "B+")]
            if da == 0:
                terms += [landing(tree, name, "ab") for name in ("A-", "A+")]
                return added(terms)
            put(tree, da, 0, "ab", terms)
            if da == 2:
                give((tree, "A2a"), tree, 2, 0, "a", (1, 0))
                give((tree, "A2b"), tree, 2, 0, "b", (-1, 0))
            else:
                name, part = ("A2a", "a") if da == 1 else ("A2b", "b")
                mine = total[cell_at(tree, da, 0), rows_of(tree, part), :]
                put(tree, da, 0, part, [mine, landing(tree, name, part)])
                give((tree, "A-" if da == 1 else "A+"), tree, da, 0, "ab", (da, 0))
        return None

    def twin_copy(step, source, cell):
        return remote(parts.at[source], twin.at[cell], back_send, back_recv, rings + step, sibling)

    def reduce_chip(at):
        dz, dy = ORDER[at]
        twin_copy(at, cell_at(0, dz, dy) * 2, cell_at(0, dz, dy)).wait_recv()
        return [reduce_item(0, dz, dy), reduce_item(1, dy, dz)]


    def backward_block(block):
        keys = shards[block, HEAD_ROWS:, 0:DH]
        values = shards[block, HEAD_ROWS:, DH:]
        key_wide = jnp.concatenate([keys, ones], axis=1)
        value_wide = jnp.concatenate([values, ones], axis=1)
        sums = []
        for head in range(HEADS):
            span = slice(head * TOK, (head + 1) * TOK)
            prob_grad = contract_last(grad_wide[head], value_wide)
            score_grad = prob[me - block, span, :].astype(F32) * prob_grad
            low = score_grad.astype(BF16)
            folded = jnp.sum(low.astype(F32).reshape(TOK // 8, 8, TOK), axis=0)
            sums.append(jnp.sum(folded, axis=0, keepdims=True))
            score_low[span, :] = low
            out_sum[head] += jnp.dot(low, key_wide, preferred_element_type=F32)
        key_part = contract_first(score_low[...], query_low[...]) * LN2
        value_part = contract_first(prob[me - block], grad_low[...])
        parts[block, HEAD_ROWS:, 0:DH] = key_part.astype(BF16)
        parts[block, HEAD_ROWS:, DH:] = value_part.astype(BF16)
        moved = (key_part * keys.astype(F32)).reshape(TOK // 8, 8, DH)
        key_gain_sum[...] += jnp.sum(moved, axis=0)
        columns = jnp.concatenate(sums + [jnp.zeros((4, TOK), F32)], axis=0)
        high = columns.astype(BF16).astype(F32)
        parts[block, 0:HEAD_ROWS, :] = jnp.concatenate([-high, high - columns], axis=0).astype(BF16)
        lane = lax.broadcasted_iota(jnp.int32, (8, DH), 1)
        whole = jnp.broadcast_to(jnp.sum(columns, axis=1, keepdims=True), (8, DH))
        offset[...] += jnp.where((lane >= block) & (lane < me), whole, 0.0)

    def backward_step(turn, _):
        step = STEPS - 1 - turn
        cell = chip_of(step)

        def one(which, _):
            block = cell * 2 + jnp.where(which == 1, core, 1 - core)
            used = (block <= me) & (block >= me - BACK)

            @pl.when(used)
            def _():
                backward_block(block)

            @pl.when(jnp.logical_not(used))
            def _():
                parts[block] = jnp.zeros((ROWS, 2 * DH), BF16)

            @pl.when(which == 0)
            def _():
                twin_copy(step, block, cell).start()

            return 0

        lax.fori_loop(0, 2, one, 0)
        for at in range(STEPS - 1, 0, -1):

            @pl.when(step == at - 1)
            def _():
                reduce_chip(at)

        return 0

    lax.fori_loop(0, STEPS, backward_step, 0)


    query_gain_sum = jnp.zeros((1, DH), F32)
    turned = []
    for head in range(HEADS):
        span = slice(head * DH, (head + 1) * DH)
        raw = query_ref[:, span].astype(F32)
        scale = lax.rsqrt(jnp.mean(raw * raw, axis=1, keepdims=True) + EPS)
        hat = raw * scale
        cotangent = out_sum[head, :, 0:DH]
        query_gain_sum += jnp.sum(cotangent * hat, axis=0, keepdims=True)
        inner = cotangent * query_scale
        mean = jnp.mean(inner * hat, axis=1, keepdims=True)
        query_grad_ref[:, span] = (scale * (inner - hat * mean)).astype(BF16)
        halves = [jnp.transpose(out_sum[head, half * DH : (half + 1) * DH, DH:])[0:1] for half in (0, 1)]
        turned.append(jnp.concatenate(halves, axis=1))
    row_sums = jnp.concatenate(turned, axis=0)
    query_gain_sum = query_gain_sum * (DH**-0.5)
    key_gain_row = jnp.sum(key_gain_sum[...], axis=0, keepdims=True) / key_gain_ref[...]
    small[0] = jnp.concatenate(
        [query_gain_sum, key_gain_row, jnp.zeros((6, DH), F32), offset[...]], axis=0
    )

    firsts = (0, 1, 4, 7)

    def small_copies(axis):
        return [
            remote(
                small.at[axis], small_landed.at[firsts[axis] + i], small_send, small_recv, firsts[axis] + i, device
            )
            for i, device in enumerate(partners[axis])
        ]

    def small_start(axis):
        for made in small_copies(axis):
            made.start()

    def small_add(axis):
        whole = small[axis]
        for i, made in enumerate(small_copies(axis)):
            made.wait_recv()
            whole = whole + small_landed[firsts[axis] + i]
        for made in small_copies(axis):
            made.wait_send()
        small[axis + 1] = whole

    small_start(0)
    finals = reduce_chip(0)
    small_add(0)
    small_start(1)

    whole = jnp.concatenate([finals[0][HEAD_ROWS:], finals[1]], axis=0)
    value_grad_ref[...] = whole[:, DH:].astype(BF16)
    cotangent = whole[:, 0:DH]
    raw = key_ref[...].astype(F32)
    scale = lax.rsqrt(jnp.mean(raw * raw, axis=1, keepdims=True) + EPS)
    hat = raw * scale
    inner = cotangent * key_gain_ref[...]
    mean = jnp.mean(inner * hat, axis=1, keepdims=True)
    key_grad_ref[...] = (scale * (inner - hat * mean)).astype(BF16)
    small_add(1)
    small_start(2)

    gates = finals[0][0:4] + finals[0][8:12] + row_sums
    row = lax.broadcasted_iota(jnp.int32, (TOK, TOK), 0)
    col = lax.broadcasted_iota(jnp.int32, (TOK, TOK), 1)
    lower = (row >= col).astype(F32)
    suffix = jnp.dot(gates, lower, preferred_element_type=F32, precision=lax.Precision.HIGHEST)
    logit = logit_ref[...].astype(F32)
    small_add(2)
    small_start(3)
    lane = lax.broadcasted_iota(jnp.int32, (4, DH), 1)
    later = jnp.sum(jnp.where(lane == me, small[3, 8:12, :], 0.0), axis=1, keepdims=True)
    forget_grad_ref[...] = (suffix + later) / (1.0 + jnp.exp(logit))
    small_add(3)
    gain_out_ref[...] = small[4, 0:2, :]

    for number, tree, part in sent:
        place = shards.at[0, rows_of(tree, part)]
        remote(place, place, out_send, out_recv, number, sibling).wait_send()
    for number, tree, name, part in back:
        goal = land(tree, name, part)
        remote(goal, goal, back_send, back_recv, number, sibling).wait_send()
    for at in range(STEPS):
        twin_copy(at, 0, 0).wait_send()
    for axis in range(3):
        for made in sum_copies(axis):
            made.wait_send()


def fused(lengths_row, key_local, value_local, logit_local, query_local, grad_local, query_gain, key_gain):
    vmem = pl.BlockSpec(memory_space=pltpu.VMEM)
    smem = pl.BlockSpec(memory_space=pltpu.SMEM)
    wide = jax.ShapeDtypeStruct((TOK, HEADS * DH), BF16)
    narrow = jax.ShapeDtypeStruct((TOK, DH), BF16)
    rows = HEADS * TOK
    dma = pltpu.SemaphoreType.DMA
    return pl.pallas_call(
        fused_kernel,
        out_shape=(
            wide,
            wide,
            narrow,
            narrow,
            jax.ShapeDtypeStruct((HEADS, TOK), F32),
            jax.ShapeDtypeStruct((2, DH), F32),
        ),
        in_specs=[smem] + [vmem] * 7,
        out_specs=(vmem,) * 6,
        scratch_shapes=[
            pltpu.VMEM((SHARDS, ROWS, 2 * DH), BF16),
            pltpu.VMEM((2, 4, 4, 8, DH), F32),
            pltpu.VMEM((SHARDS, 8, DH), F32),
            pltpu.VMEM((HEADS, TOK, 2 * DH), BF16),
            pltpu.VMEM((rows, DH), BF16),
            pltpu.VMEM((HEADS, TOK, 2 * DH), BF16),
            pltpu.VMEM((rows, DH), BF16),
            pltpu.VMEM((BACK + 1, rows, TOK), BF16),
            pltpu.VMEM((rows, TOK), BF16),
            pltpu.VMEM((HEADS, TOK, 2 * DH), F32),
            pltpu.VMEM((8, DH), F32),
            pltpu.VMEM((8, DH), F32),
            pltpu.VMEM((SHARDS, ROWS, 2 * DH), BF16),
            pltpu.VMEM((SHARDS // 2, ROWS, 2 * DH), BF16),
            pltpu.VMEM((SHARDS // 2, ROWS, 2 * DH), BF16),
            pltpu.VMEM((40, PIECES[1][1], 2 * DH), BF16),
            pltpu.VMEM((5, 16, DH), F32),
            pltpu.VMEM((10, 16, DH), F32),
            dma((40 + 2 * STEPS,)),
            dma((40 + 2 * STEPS,)),
            dma((40 + STEPS,)),
            dma((40 + STEPS,)),
            dma((7,)),
            dma((7,)),
            dma((10,)),
            dma((10,)),
        ],
        compiler_params=pltpu.CompilerParams(
            collective_id=0, has_side_effects=True, vmem_limit_bytes=56 * 2**20
        ),
        name="attend_whole",
    )(lengths_row, key_local, value_local, logit_local, query_local, grad_local, query_gain, key_gain)


def on_device(queries, key_vectors, values, forget_logit, out_grad, query_gain, key_gain, lengths):
    attention, query_grad, key_grad, value_grad, forget_grad, gain_grad = fused(
        lengths[0],
        key_vectors[0],
        values[0],
        forget_logit[0],
        queries[0],
        out_grad[0],
        query_gain.reshape(1, DH),
        key_gain.reshape(1, DH),
    )
    return (
        attention[None],
        query_grad[None],
        key_grad[None],
        value_grad[None],
        forget_grad[None],
        gain_grad,
    )


def solution(mesh):
    return jax.shard_map(
        on_device,
        mesh=mesh,
        in_specs=(
            P("rep", "seq", None),
            P("rep", "seq", None),
            P("rep", "seq", None),
            P("rep", None, "seq"),
            P("rep", "seq", None),
            P(),
            P(),
            P("rep", None),
        ),
        out_specs=(
            P("rep", "seq", None),
            P("rep", "seq", None),
            P("rep", "seq", None),
            P("rep", "seq", None),
            P("rep", None, "seq"),
            P(),
        ),
        check_vma=False,
    )
```

```python
import functools
import math

import jax
import jax.numpy as jnp
from jax import lax
from jax.experimental import pallas as pl
from jax.experimental.pallas import tpu as pltpu
from jax.sharding import PartitionSpec as P

MESH = pl.DeviceIdType.MESH
F32 = jnp.float32
BF16 = jnp.bfloat16

EPS = 1e-06
HEADS = 4
DH = 128
TOK = 256
TILE = 64
SHARDS = 32
HEAD_ROWS = 16
ROWS = HEAD_ROWS + TOK
PIECES = ((0, 80), (80, 144), (144, 208), (208, 272))
LOG2E = math.log2(math.e)
LN2 = math.log(2.0)
FAR = (2, -1, 1, 0)
BACK = 24
ORDER = (
    (0, 0), (-1, 0), (0, -1), (1, 0), (0, 1), (-1, -1), (-1, 1), (1, -1),
    (1, 1), (2, 0), (0, 2), (2, -1), (-1, 2), (2, 1), (1, 2), (2, 2),
)
STEPS = len(ORDER)
LATE = (
    (4, (1, 2, 1)), (4, (0, 2, 1)), (5, (1, 2, -1)), (6, (0, 2, -1)), (9, (1, 2, 0)), (9, (0, 2, 0)),
)


def piece(tree, part):
    low, high = PIECES[2 * tree], PIECES[2 * tree + 1]
    first, last = {"a": low, "b": high, "ab": (low[0], high[1])}[part]
    return first, last - first


def rows_of(tree, part):
    first, count = piece(tree, part)
    return pl.ds(first, count)


def greet(devices):
    barrier = pltpu.get_barrier_semaphore()
    for device in devices:
        pl.semaphore_signal(barrier, inc=1, device_id=device, device_id_type=MESH)
    pl.semaphore_wait(barrier, len(devices))


def ring_events():
    names = ["A-", "A+", "A2a", "A2b"]
    for da in FAR:
        names += [("B-", da), ("B+", da), ("B2a", da), ("B2b", da)]
    return names


def split3(x):
    high = x.astype(BF16)
    rest = x - high.astype(F32)
    mid = rest.astype(BF16)
    low = (rest - mid.astype(F32)).astype(BF16)
    return high, mid, low


def row_to_columns(row):
    parts = [
        jnp.transpose(jnp.broadcast_to(row[:, half * DH : (half + 1) * DH], (DH, DH)))
        for half in (0, 1)
    ]
    return jnp.concatenate(parts, axis=0)


def turn(x):
    if x.shape[0] == DH:
        return jnp.concatenate([jnp.transpose(x[:, :DH]), jnp.transpose(x[:, DH:])], axis=0)
    return jnp.concatenate([jnp.transpose(x[:DH]), jnp.transpose(x[DH:])], axis=1)


def split_lanes(full):
    high, mid, low = split3(full)
    lane = lax.broadcasted_iota(jnp.int32, full.shape, 1)
    picked = jnp.where(
        lane == 0,
        high.astype(F32),
        jnp.where(lane == 1, mid.astype(F32), jnp.where(lane == 2, low.astype(F32), 0.0)),
    )
    return picked.astype(BF16)


def contract_last(left, right):
    return lax.dot_general(left, right, (((1,), (1,)), ((), ())), preferred_element_type=F32)


def pick(step, entries):
    found = entries[0]
    for i, entry in enumerate(entries):
        if i:
            found = jnp.where(step == i, entry, found)
    return found


def step_of(tree, da, db):
    return ORDER.index((da, db) if tree == 0 else (db, da))


def fused_kernel(
    length_ref,
    key_ref,
    value_ref,
    logit_ref,
    query_ref,
    grad_ref,
    query_gain_ref,
    key_gain_ref,
    att_ref,
    query_grad_ref,
    key_grad_ref,
    value_grad_ref,
    forget_grad_ref,
    gain_out_ref,
    shards,
    chunk_sum,
    base,
    query_wide,
    query_turned,
    grad_wide,
    grad_turned,
    prob,
    score_low,
    out_sum,
    key_gain_sum,
    offset,
    parts,
    twin,
    total,
    landed,
    small,
    small_landed,
    out_send,
    out_recv,
    back_send,
    back_recv,
    sum_send,
    sum_recv,
    small_send,
    small_recv,
):
    me, rep = lax.axis_index("seq"), lax.axis_index("rep")
    z, y, core = me // 8, (me // 2) % 4, me % 2
    zs, ys, reps = (
        {step: at if step == 0 else (at + (step + 4) % 4) % 4 for step in range(-3, 4)} for at in (z, y, rep)
    )
    cells = {(dz, dy): zs[dz] * 4 + ys[dy] for dz in FAR for dy in FAR}
    places = {key: cell * 2 + core for key, cell in cells.items()}
    other = 1 - core

    def cell_at(tree, da, db):
        return cells[(da, db) if tree == 0 else (db, da)]

    def shard_at(tree, da, db):
        return places[(da, db) if tree == 0 else (db, da)]

    def device_at(tree, da, db):
        return (shard_at(tree, da, db), rep)

    sibling = (z * 8 + y * 2 + other, rep)
    line_steps = [(dz, dc) for dz in range(4) for dc in range(2) if dz or dc]
    field_steps = [(dy, dx) for dy in range(4) for dx in range(4) if dy or dx]
    partners = [
        [(zs[dz] * 8 + y * 2 + (other if dc else core), rep) for dz, dc in line_steps],
        [(z * 8 + ys[dy] * 2 + core, reps[dx]) for dy, dx in field_steps],
    ]
    greet([device for group in partners for device in group])

    def remote(source, target, sends, receives, number, device):
        return pltpu.make_async_remote_copy(
            src_ref=source,
            dst_ref=target,
            send_sem=sends.at[number],
            recv_sem=receives.at[number],
            device_id=device,
            device_id_type=MESH,
        )


    raw = key_ref[...].astype(F32)
    scale = lax.rsqrt(jnp.mean(raw * raw, axis=1, keepdims=True) + EPS)
    shards[me, HEAD_ROWS:, 0:DH] = (raw * scale * key_gain_ref[...]).astype(BF16)
    shards[me, HEAD_ROWS:, DH:] = value_ref[...]
    logit = logit_ref[...].astype(F32)
    decay = jnp.minimum(logit, 0.0) - jnp.log1p(jnp.exp(-jnp.abs(logit)))
    row = lax.broadcasted_iota(jnp.int32, (TOK, TOK), 0)
    col = lax.broadcasted_iota(jnp.int32, (TOK, TOK), 1)
    upper = (row <= col).astype(F32)
    local = jnp.dot(decay, upper, preferred_element_type=F32, precision=lax.Precision.HIGHEST)
    local = local * LOG2E
    high = local.astype(BF16).astype(F32)
    mid = (local - high).astype(BF16).astype(F32)
    packed = [high, mid, local - high - mid, jnp.zeros((4, TOK), F32)]
    shards[me, 0:HEAD_ROWS, :] = jnp.concatenate(packed, axis=0).astype(BF16)

    ids = {}
    for tree in (0, 1):
        for name in ring_events():
            ids[tree, name] = len(ids)
    rings = len(ids)


    sent = []

    def send(event, tree, da, db, part, target):
        place = shards.at[shard_at(tree, da, db), rows_of(tree, part)]
        device = device_at(tree, *target)
        remote(place, place, out_send, out_recv, ids[event], device).start()
        sent.append((ids[event], tree, part))

    def share(tree, da, db):
        place = shards.at[shard_at(tree, da, db), rows_of(tree, "ab")]
        number = rings + 2 * step_of(tree, da, db) + tree
        remote(place, place, out_send, out_recv, number, sibling).start()
        sent.append((number, tree, "ab"))

    def wait(tree, name, da, db, part):
        place = shards.at[shard_at(tree, da, db), rows_of(tree, part)]
        remote(place, place, out_send, out_recv, ids[tree, name], sibling).wait_recv()

    for tree in (0, 1):
        send((tree, "A-"), tree, 0, 0, "ab", (1, 0))
        send((tree, "A+"), tree, 0, 0, "ab", (-1, 0))

    line = z * 2 + core
    chunk_sum[y, line] = jnp.concatenate(
        [jnp.broadcast_to(local[:, TOK - 1 :], (4, DH)), jnp.zeros((4, DH), F32)], axis=0
    )

    def sum_copies(axis):
        if axis == 0:
            place, devices = chunk_sum.at[y, line], partners[0]
        else:
            place = chunk_sum.at[y]
            devices = [(z * 8 + ys[step] * 2 + core, rep) for step in (1, 2, 3)]
        return [
            remote(place, place, sum_send, sum_recv, 7 * axis + i, device)
            for i, device in enumerate(devices)
        ]

    def sum_wait(axis):
        for i in range(3 if axis else 7):
            if axis == 0:
                dz, dc = line_steps[i]
                place = chunk_sum.at[y, zs[-dz] * 2 + (other if dc else core)]
            else:
                place = chunk_sum.at[ys[-i - 1]]
            remote(place, place, sum_send, sum_recv, 7 * axis + i, sibling).wait_recv()

    for made in sum_copies(0):
        made.start()
    for tree in (0, 1):
        send((tree, ("B-", 0)), tree, 0, 0, "ab", (0, 1))
        send((tree, ("B+", 0)), tree, 0, 0, "ab", (0, -1))
        share(tree, 0, 0)

    def axis_near():
        for tree in (0, 1):
            wait(tree, "A-", -1, 0, "ab")
            send((tree, "A2a"), tree, -1, 0, "a", (1, 0))
            wait(tree, "A+", 1, 0, "ab")
            send((tree, "A2b"), tree, 1, 0, "b", (-1, 0))
            for da in (-1, 1):
                send((tree, ("B-", da)), tree, da, 0, "ab", (0, 1))
                send((tree, ("B+", da)), tree, da, 0, "ab", (0, -1))
                share(tree, da, 0)

    def axis_far():
        for tree in (0, 1):
            wait(tree, "A2a", 2, 0, "a")
            wait(tree, "A2b", 2, 0, "b")
            send((tree, ("B-", 2)), tree, 2, 0, "ab", (0, 1))
            send((tree, ("B+", 2)), tree, 2, 0, "ab", (0, -1))
            share(tree, 2, 0)

    def near(da):
        for tree in (0, 1):
            wait(tree, ("B-", da), da, -1, "ab")
            send((tree, ("B2a", da)), tree, da, -1, "a", (0, 1))
            wait(tree, ("B+", da), da, 1, "ab")
            send((tree, ("B2b", da)), tree, da, 1, "b", (0, -1))
            share(tree, da, -1)
            share(tree, da, 1)

    def far(da):
        for tree in (0, 1):
            wait(tree, ("B2a", da), da, 2, "a")
            wait(tree, ("B2b", da), da, 2, "b")
            share(tree, da, 2)

    gather_steps = {
        0: axis_far,
        1: functools.partial(near, -1),
        2: functools.partial(near, 1),
        3: functools.partial(far, 0),
        4: functools.partial(near, 2),
        5: functools.partial(far, -1),
        6: functools.partial(far, 1),
        7: functools.partial(far, 2),
    }


    ones = jnp.ones((TOK, DH), BF16)
    starts = []
    for tile in range(TOK // TILE):
        at = me * (TOK // TILE) + tile
        end = jnp.int32(0)
        start = jnp.int32(0)
        for document in range(4):
            end = end + length_ref[document]
            start = jnp.where(end <= at, end, start)
        starts.append(start * TILE)
    query_scale = query_gain_ref[...] * (DH**-0.5)
    for head in range(HEADS):
        raw = query_ref[:, head * DH : (head + 1) * DH].astype(F32)
        scale = lax.rsqrt(jnp.mean(raw * raw, axis=1, keepdims=True) + EPS)
        normed = (raw * scale * (query_scale * LOG2E)).astype(BF16)
        own_gate = row_to_columns(local[head : head + 1, :])
        query_turned[:, head * TOK : (head + 1) * TOK] = turn(normed.astype(F32)).astype(BF16)
        query_wide[head] = jnp.concatenate([normed, split_lanes(own_gate)], axis=1)
    out_sum[...] = jnp.zeros_like(out_sum)
    key_gain_sum[...] = jnp.zeros_like(key_gain_sum)
    offset[...] = jnp.zeros_like(offset)
    lane_token = lax.broadcasted_iota(jnp.int32, (1, TOK), 1)

    def forward_block(block, diagonal):
        keys = shards[block, HEAD_ROWS:, 0:DH]
        values = shards[block, HEAD_ROWS:, DH:]
        key_wide = jnp.concatenate([keys, ones], axis=1)
        value_wide = jnp.concatenate([values, ones], axis=1)
        token = block * TOK + lane_token
        packed = shards[block, 0:HEAD_ROWS, :].astype(F32)
        gate = packed[0:4] + packed[4:8] + packed[8:12]
        if not diagonal:
            before = base[block, 0:4, :]
            gate = gate + jnp.concatenate([before, before], axis=1)
        following = contract_last(query_wide[0], key_wide)
        for head in range(HEADS):
            scores = following
            if head + 1 < HEADS:
                following = contract_last(query_wide[head + 1], key_wide)
            pieces = []
            for tile in range(TOK // TILE):
                low = jnp.where(token >= starts[tile], gate[head : head + 1], jnp.inf)
                pieces.append(scores[tile * TILE : (tile + 1) * TILE] - low)
            scores = jnp.concatenate(pieces, axis=0)
            if diagonal:
                row = lax.broadcasted_iota(jnp.int32, (TOK, TOK), 0)
                col = lax.broadcasted_iota(jnp.int32, (TOK, TOK), 1)
                scores = jnp.where(col <= row, scores, -jnp.inf)
            weights = jnp.exp2(scores).astype(BF16)
            prob[me - block, head * TOK : (head + 1) * TOK, :] = weights
            out_sum[head] += jnp.dot(weights, value_wide, preferred_element_type=F32)

    forward_block(me, True)
    sum_wait(0)
    for made in sum_copies(1):
        made.start()
    axis_near()
    near(0)
    sum_wait(1)

    carry = jnp.zeros((8, DH), F32)
    for shard in range(SHARDS - 1, -1, -1):
        chunk = chunk_sum[(shard // 2) % 4, (shard // 8) * 2 + shard % 2]
        carry = carry - jnp.where(shard < me, chunk, 0.0)
        base[shard] = carry

    def chip_of(step):
        return pick(step, [cells[entry] for entry in ORDER])

    def forward_step(step, _):
        cell = chip_of(step)

        for at, action in gather_steps.items():
            pl.when(step == at)(action)

        def one(which, _):
            block = cell * 2 + jnp.where(which == 0, core, 1 - core)

            @pl.when(which == 1)
            def _():
                for tree in (0, 1):
                    place = shards.at[block, rows_of(tree, "ab")]
                    number = rings + 2 * step + tree
                    remote(place, place, out_send, out_recv, number, sibling).wait_recv()

            @pl.when((block < me) & (block >= me - BACK))
            def _():
                forward_block(block, False)

            return 0

        return lax.fori_loop(0, 2, one, 0)

    lax.fori_loop(0, STEPS, forward_step, 0)

    for head in range(HEADS):
        span = slice(head * DH, (head + 1) * DH)
        inverse = 1.0 / out_sum[head, :, DH:]
        out = out_sum[head, :, 0:DH] * inverse
        att_ref[:, span] = out.astype(BF16)
        scaled = (grad_ref[:, span].astype(F32) * inverse).astype(BF16)
        inner = jnp.sum(scaled.astype(F32) * out, axis=1, keepdims=True)
        grad_turned[:, head * TOK : (head + 1) * TOK] = turn(scaled.astype(F32)).astype(BF16)
        grad_wide[head] = jnp.concatenate(
            [scaled, split_lanes(jnp.broadcast_to(-inner, (TOK, DH)))], axis=1
        )
    out_sum[...] = jnp.zeros_like(out_sum)


    back = []

    def land(tree, name, part):
        first, count = piece(tree, part)
        return landed.at[ids[tree, name], pl.ds(first - piece(tree, "ab")[0], count)]

    def give(event, tree, da, db, part, target):
        source = total.at[cell_at(tree, da, db), rows_of(tree, part)]
        device = device_at(tree, *target)
        goal = land(event[0], event[1], part)
        remote(source, goal, back_send, back_recv, ids[event], device).start()
        back.append((ids[event], event[0], event[1], part))

    def landing(tree, name, part):
        goal = land(tree, name, part)
        remote(goal, goal, back_send, back_recv, ids[tree, name], sibling).wait_recv()
        return goal[...]

    def added(terms):
        return functools.reduce(lambda a, b: a + b, [term.astype(F32) for term in terms])

    def put(tree, da, db, part, terms):
        whole = added(terms)
        if tree == 0 and part in ("a", "ab"):
            gates = whole[0:8] + whole[8:16]
            high = gates.astype(BF16).astype(F32)
            whole = jnp.concatenate([high, gates - high, whole[16:]], axis=0)
        total[cell_at(tree, da, db), rows_of(tree, part), :] = whole.astype(BF16)

    def twins(tree, da, db, part):
        place, rows = cell_at(tree, da, db), rows_of(tree, part)
        return [parts[shard_at(tree, da, db), rows, :], twin[place, rows, :]]

    def reduce_item(tree, da, db):
        if db == 2:
            put(tree, da, 2, "ab", twins(tree, da, 2, "ab"))
            give((tree, ("B2a", da)), tree, da, 2, "a", (0, 1))
            give((tree, ("B2b", da)), tree, da, 2, "b", (0, -1))
        elif db in (1, -1):
            name, close, away = ("B2a", "a", "b") if db == 1 else ("B2b", "b", "a")
            put(tree, da, db, away, twins(tree, da, db, away))
            put(tree, da, db, close, twins(tree, da, db, close) + [landing(tree, (name, da), close)])
            give((tree, ("B-" if db == 1 else "B+", da)), tree, da, db, "ab", (0, db))
        else:
            terms = twins(tree, da, 0, "ab")
            terms += [landing(tree, (name, da), "ab") for name in ("B-", "B+")]
            if da == 0:
                terms += [landing(tree, name, "ab") for name in ("A-", "A+")]
                return added(terms)
            put(tree, da, 0, "ab", terms)
            if da == 2:
                give((tree, "A2a"), tree, 2, 0, "a", (1, 0))
                give((tree, "A2b"), tree, 2, 0, "b", (-1, 0))
            else:
                name, part = ("A2a", "a") if da == 1 else ("A2b", "b")
                mine = total[cell_at(tree, da, 0), rows_of(tree, part), :]
                put(tree, da, 0, part, [mine, landing(tree, name, part)])
                give((tree, "A-" if da == 1 else "A+"), tree, da, 0, "ab", (da, 0))
        return None

    def twin_copy(step, source, cell):
        return remote(parts.at[source], twin.at[cell], back_send, back_recv, rings + step, sibling)

    def reduce_turn(turn):
        at = STEPS - turn
        dz, dy = ORDER[at]
        twin_copy(at, cell_at(0, dz, dy) * 2, cell_at(0, dz, dy)).wait_recv()
        items = [(0, dz, dy), (1, dy, dz)]
        now = [item for item in items if item not in [late for _, late in LATE]]
        now += [late for when, late in LATE if when == turn]
        return [reduce_item(*item) for item in now]


    def backward_block(block):
        keys = shards[block, HEAD_ROWS:, 0:DH]
        values = shards[block, HEAD_ROWS:, DH:]
        key_wide = jnp.concatenate([keys, ones], axis=1)
        value_wide = jnp.concatenate([values, ones], axis=1)
        sums = []
        following = contract_last(grad_wide[0], value_wide)
        for head in range(HEADS):
            span = slice(head * TOK, (head + 1) * TOK)
            prob_grad = following
            if head + 1 < HEADS:
                following = contract_last(grad_wide[head + 1], value_wide)
            score_grad = prob[me - block, span, :].astype(F32) * prob_grad
            low = score_grad.astype(BF16)
            folded = jnp.sum(low.astype(F32).reshape(TOK // 8, 8, TOK), axis=0)
            sums.append(jnp.sum(folded, axis=0, keepdims=True))
            score_low[span, :] = low
            out_sum[head] += jnp.dot(low, key_wide, preferred_element_type=F32)
        key_part = (jnp.dot(query_turned[...], score_low[...], preferred_element_type=F32) * LN2).astype(BF16)
        value_part = jnp.dot(grad_turned[...], prob[me - block], preferred_element_type=F32)
        parts[block, HEAD_ROWS : HEAD_ROWS + DH, :] = key_part
        parts[block, HEAD_ROWS + DH :, :] = value_part.astype(BF16)
        key_gain_sum[...] += jnp.dot(key_part, keys, preferred_element_type=F32)
        columns = jnp.concatenate(sums + [jnp.zeros((4, TOK), F32)], axis=0)
        high = columns.astype(BF16).astype(F32)
        parts[block, 0:HEAD_ROWS, :] = jnp.concatenate([-high, high - columns], axis=0).astype(BF16)
        lane = lax.broadcasted_iota(jnp.int32, (8, DH), 1)
        whole = jnp.broadcast_to(jnp.sum(columns, axis=1, keepdims=True), (8, DH))
        offset[...] += jnp.where((lane >= block) & (lane < me), whole, 0.0)

    def backward_step(turn, _):
        step = STEPS - 1 - turn
        cell = chip_of(step)

        def one(which, _):
            block = cell * 2 + jnp.where(which == 1, core, 1 - core)
            used = (block <= me) & (block >= me - BACK)

            @pl.when(used)
            def _():
                backward_block(block)

            @pl.when(jnp.logical_not(used))
            def _():
                parts[block] = jnp.zeros((ROWS, 2 * DH), BF16)

            @pl.when(which == 0)
            def _():
                twin_copy(step, block, cell).start()

            return 0

        lax.fori_loop(0, 2, one, 0)
        for at in range(1, STEPS):

            @pl.when(turn == at)
            def _():
                reduce_turn(at)

        return 0

    lax.fori_loop(0, STEPS, backward_step, 0)


    query_gain_sum = jnp.zeros((1, DH), F32)
    turned = []
    for head in range(HEADS):
        span = slice(head * DH, (head + 1) * DH)
        raw = query_ref[:, span].astype(F32)
        scale = lax.rsqrt(jnp.mean(raw * raw, axis=1, keepdims=True) + EPS)
        hat = raw * scale
        cotangent = out_sum[head, :, 0:DH]
        query_gain_sum += jnp.sum(cotangent * hat, axis=0, keepdims=True)
        inner = cotangent * query_scale
        mean = jnp.mean(inner * hat, axis=1, keepdims=True)
        query_grad_ref[:, span] = (scale * (inner - hat * mean)).astype(BF16)
        halves = [jnp.transpose(out_sum[head, half * DH : (half + 1) * DH, DH:])[0:1] for half in (0, 1)]
        turned.append(jnp.concatenate(halves, axis=1))
    row_sums = jnp.concatenate(turned, axis=0)
    query_gain_sum = query_gain_sum * (DH**-0.5)
    row = lax.broadcasted_iota(jnp.int32, (DH, DH), 0)
    col = lax.broadcasted_iota(jnp.int32, (DH, DH), 1)
    diagonal = jnp.where(row == col, key_gain_sum[...], 0.0)
    key_gain_row = jnp.sum(diagonal, axis=0, keepdims=True) / key_gain_ref[...]
    small[0] = jnp.concatenate(
        [query_gain_sum, key_gain_row, jnp.zeros((6, DH), F32), offset[...]], axis=0
    )

    def small_copies(axis):
        return [
            remote(small.at[axis], small_landed.at[7 * axis + i], small_send, small_recv, 7 * axis + i, device)
            for i, device in enumerate(partners[axis])
        ]

    def small_add(axis):
        whole = small[axis]
        shared = lax.broadcasted_iota(jnp.int32, (16, DH), 0) < 8
        for i, made in enumerate(small_copies(axis)):
            made.wait_recv()
            term = small_landed[7 * axis + i]
            if axis == 1 and field_steps[i][1]:
                term = jnp.where(shared, term, 0.0)
            whole = whole + term
        small[axis + 1] = whole

    for made in small_copies(0):
        made.start()
    finals = reduce_turn(STEPS)
    small_add(0)
    for made in small_copies(1):
        made.start()

    value_grad_ref[...] = turn(finals[1]).astype(BF16)
    cotangent = turn(finals[0][HEAD_ROWS:])
    raw = key_ref[...].astype(F32)
    scale = lax.rsqrt(jnp.mean(raw * raw, axis=1, keepdims=True) + EPS)
    hat = raw * scale
    inner = cotangent * key_gain_ref[...]
    mean = jnp.mean(inner * hat, axis=1, keepdims=True)
    key_grad_ref[...] = (scale * (inner - hat * mean)).astype(BF16)

    gates = finals[0][0:4] + finals[0][8:12] + row_sums
    row = lax.broadcasted_iota(jnp.int32, (TOK, TOK), 0)
    col = lax.broadcasted_iota(jnp.int32, (TOK, TOK), 1)
    lower = (row >= col).astype(F32)
    suffix = jnp.dot(gates, lower, preferred_element_type=F32, precision=lax.Precision.HIGHEST)
    logit = logit_ref[...].astype(F32)
    small_add(1)
    lane = lax.broadcasted_iota(jnp.int32, (4, DH), 1)
    later = jnp.sum(jnp.where(lane == me, small[2, 8:12, :], 0.0), axis=1, keepdims=True)
    forget_grad_ref[...] = (suffix + later) / (1.0 + jnp.exp(logit))
    gain_out_ref[...] = small[2, 0:2, :]

    for number, tree, part in sent:
        place = shards.at[0, rows_of(tree, part)]
        remote(place, place, out_send, out_recv, number, sibling).wait_send()
    for number, tree, name, part in back:
        goal = land(tree, name, part)
        remote(goal, goal, back_send, back_recv, number, sibling).wait_send()
    for at in range(STEPS):
        twin_copy(at, 0, 0).wait_send()
    for axis in range(2):
        for made in sum_copies(axis) + small_copies(axis):
            made.wait_send()


def fused(lengths_row, key_local, value_local, logit_local, query_local, grad_local, query_gain, key_gain):
    vmem = pl.BlockSpec(memory_space=pltpu.VMEM)
    smem = pl.BlockSpec(memory_space=pltpu.SMEM)
    wide = jax.ShapeDtypeStruct((TOK, HEADS * DH), BF16)
    narrow = jax.ShapeDtypeStruct((TOK, DH), BF16)
    rows = HEADS * TOK
    dma = pltpu.SemaphoreType.DMA
    return pl.pallas_call(
        fused_kernel,
        out_shape=(
            wide,
            wide,
            narrow,
            narrow,
            jax.ShapeDtypeStruct((HEADS, TOK), F32),
            jax.ShapeDtypeStruct((2, DH), F32),
        ),
        in_specs=[smem] + [vmem] * 7,
        out_specs=(vmem,) * 6,
        scratch_shapes=[
            pltpu.VMEM((SHARDS, ROWS, 2 * DH), BF16),
            pltpu.VMEM((4, 8, 8, DH), F32),
            pltpu.VMEM((SHARDS, 8, DH), F32),
            pltpu.VMEM((HEADS, TOK, 2 * DH), BF16),
            pltpu.VMEM((DH, rows), BF16),
            pltpu.VMEM((HEADS, TOK, 2 * DH), BF16),
            pltpu.VMEM((DH, rows), BF16),
            pltpu.VMEM((BACK + 1, rows, TOK), BF16),
            pltpu.VMEM((rows, TOK), BF16),
            pltpu.VMEM((HEADS, TOK, 2 * DH), F32),
            pltpu.VMEM((DH, DH), F32),
            pltpu.VMEM((8, DH), F32),
            pltpu.VMEM((SHARDS, ROWS, 2 * DH), BF16),
            pltpu.VMEM((SHARDS // 2, ROWS, 2 * DH), BF16),
            pltpu.VMEM((SHARDS // 2, ROWS, 2 * DH), BF16),
            pltpu.VMEM((40, PIECES[1][1], 2 * DH), BF16),
            pltpu.VMEM((3, 16, DH), F32),
            pltpu.VMEM((22, 16, DH), F32),
            dma((40 + 2 * STEPS,)),
            dma((40 + 2 * STEPS,)),
            dma((40 + STEPS,)),
            dma((40 + STEPS,)),
            dma((10,)),
            dma((10,)),
            dma((22,)),
            dma((22,)),
        ],
        compiler_params=pltpu.CompilerParams(
            collective_id=0, has_side_effects=True, vmem_limit_bytes=56 * 2**20
        ),
        name="attend_whole",
    )(lengths_row, key_local, value_local, logit_local, query_local, grad_local, query_gain, key_gain)


def write_kernel(*refs):
    count = len(refs) // 2
    for i in range(count):
        refs[count + i][...] = refs[i][...]


def write(*arrays):
    vmem = pl.BlockSpec(memory_space=pltpu.VMEM)
    return pl.pallas_call(
        write_kernel,
        out_shape=tuple(jax.ShapeDtypeStruct(a.shape, a.dtype) for a in arrays),
        in_specs=[vmem] * len(arrays),
        out_specs=(vmem,) * len(arrays),
        name="write_results",
    )(*arrays)


def on_device(queries, key_vectors, values, forget_logit, out_grad, query_gain, key_gain, lengths):
    results = fused(
        lengths[0],
        key_vectors[0],
        values[0],
        forget_logit[0],
        queries[0],
        out_grad[0],
        query_gain.reshape(1, DH),
        key_gain.reshape(1, DH),
    )
    attention, query_grad, key_grad, value_grad, forget_grad, gain_grad = write(*results)
    return (
        attention[None],
        query_grad[None],
        key_grad[None],
        value_grad[None],
        forget_grad[None],
        gain_grad,
    )


def solution(mesh):
    return jax.shard_map(
        on_device,
        mesh=mesh,
        in_specs=(
            P("rep", "seq", None),
            P("rep", "seq", None),
            P("rep", "seq", None),
            P("rep", None, "seq"),
            P("rep", "seq", None),
            P(),
            P(),
            P("rep", None),
        ),
        out_specs=(
            P("rep", "seq", None),
            P("rep", "seq", None),
            P("rep", "seq", None),
            P("rep", "seq", None),
            P("rep", None, "seq"),
            P(),
        ),
        check_vma=False,
    )
```

```python
import functools
import math

import jax
import jax.numpy as jnp
from jax import lax
from jax.experimental import pallas as pl
from jax.experimental.pallas import tpu as pltpu
from jax.sharding import PartitionSpec as P

MESH = pl.DeviceIdType.MESH
F32 = jnp.float32
BF16 = jnp.bfloat16

EPS = 1e-06
HEADS = 4
DH = 128
TOK = 256
TILE = 64
SHARDS = 32
HEAD_ROWS = 16
ROWS = HEAD_ROWS + TOK
PIECES = ((0, 80), (80, 144), (144, 208), (208, 272))
LOG2E = math.log2(math.e)
LN2 = math.log(2.0)
FAR = (2, -1, 1, 0)
BACK = 24
FORWARD = (
    (0, 0), (-1, 0), (0, -1), (1, 0), (0, 1), (2, 0), (0, 2), (-1, -1),
    (-1, 1), (1, -1), (1, 1), (2, -1), (-1, 2), (2, 1), (1, 2), (2, 2),
)
ORDER = (
    (0, 0), (-1, 0), (0, -1), (1, 0), (0, 1), (-1, -1), (-1, 1), (1, -1),
    (1, 1), (2, 0), (0, 2), (2, -1), (-1, 2), (2, 1), (1, 2), (2, 2),
)
STEPS = len(ORDER)
LATE = (
    (4, (1, 2, 1)), (4, (0, 2, 1)), (5, (1, 2, -1)), (6, (0, 2, -1)), (9, (1, 2, 0)), (9, (0, 2, 0)),
)


def piece(tree, part):
    low, high = PIECES[2 * tree], PIECES[2 * tree + 1]
    first, last = {"a": low, "b": high, "ab": (low[0], high[1])}[part]
    return first, last - first


def rows_of(tree, part):
    first, count = piece(tree, part)
    return pl.ds(first, count)


def greet(devices):
    barrier = pltpu.get_barrier_semaphore()
    for device in devices:
        pl.semaphore_signal(barrier, inc=1, device_id=device, device_id_type=MESH)
    pl.semaphore_wait(barrier, len(devices))


def ring_events():
    names = ["A-", "A+", "A2a", "A2b"]
    for da in FAR:
        names += [("B-", da), ("B+", da), ("B2a", da), ("B2b", da)]
    return names


def split3(x):
    high = x.astype(BF16)
    rest = x - high.astype(F32)
    mid = rest.astype(BF16)
    low = (rest - mid.astype(F32)).astype(BF16)
    return high, mid, low


def row_to_columns(row):
    parts = [
        jnp.transpose(jnp.broadcast_to(row[:, half * DH : (half + 1) * DH], (DH, DH)))
        for half in (0, 1)
    ]
    return jnp.concatenate(parts, axis=0)


def turn(x):
    if x.shape[0] == DH:
        return jnp.concatenate([jnp.transpose(x[:, :DH]), jnp.transpose(x[:, DH:])], axis=0)
    return jnp.concatenate([jnp.transpose(x[:DH]), jnp.transpose(x[DH:])], axis=1)


def split_lanes(full):
    high, mid, low = split3(full)
    lane = lax.broadcasted_iota(jnp.int32, full.shape, 1)
    picked = jnp.where(
        lane == 0,
        high.astype(F32),
        jnp.where(lane == 1, mid.astype(F32), jnp.where(lane == 2, low.astype(F32), 0.0)),
    )
    return picked.astype(BF16)


def contract_last(left, right):
    return lax.dot_general(left, right, (((1,), (1,)), ((), ())), preferred_element_type=F32)


def pick(step, entries):
    found = entries[0]
    for i, entry in enumerate(entries):
        if i:
            found = jnp.where(step == i, entry, found)
    return found


def step_of(tree, da, db):
    return FORWARD.index((da, db) if tree == 0 else (db, da))


def fused_kernel(
    length_ref,
    key_ref,
    value_ref,
    logit_ref,
    query_ref,
    grad_ref,
    query_gain_ref,
    key_gain_ref,
    att_ref,
    query_grad_ref,
    key_grad_ref,
    value_grad_ref,
    forget_grad_ref,
    gain_out_ref,
    shards,
    chunk_sum,
    base,
    query_wide,
    query_turned,
    grad_wide,
    grad_turned,
    prob,
    score_low,
    out_sum,
    offset,
    parts,
    twin,
    total,
    landed,
    small,
    small_landed,
    out_send,
    out_recv,
    back_send,
    back_recv,
    sum_send,
    sum_recv,
    small_send,
    small_recv,
):
    me, rep = lax.axis_index("seq"), lax.axis_index("rep")
    z, y, core = me // 8, (me // 2) % 4, me % 2
    zs, ys, reps = (
        {step: at if step == 0 else (at + (step + 4) % 4) % 4 for step in range(-3, 4)} for at in (z, y, rep)
    )
    cells = {(dz, dy): zs[dz] * 4 + ys[dy] for dz in FAR for dy in FAR}
    places = {key: cell * 2 + core for key, cell in cells.items()}
    other = 1 - core

    def cell_at(tree, da, db):
        return cells[(da, db) if tree == 0 else (db, da)]

    def shard_at(tree, da, db):
        return places[(da, db) if tree == 0 else (db, da)]

    def device_at(tree, da, db):
        return (shard_at(tree, da, db), rep)

    sibling = (z * 8 + y * 2 + other, rep)
    line_steps = [(dz, dc) for dz in range(4) for dc in range(2) if dz or dc]
    field_steps = [(dy, dx) for dy in range(4) for dx in range(4) if dy or dx]
    partners = [
        [(zs[dz] * 8 + y * 2 + (other if dc else core), rep) for dz, dc in line_steps],
        [(z * 8 + ys[dy] * 2 + core, reps[dx]) for dy, dx in field_steps],
    ]
    greet([device for group in partners for device in group])

    def remote(source, target, sends, receives, number, device):
        return pltpu.make_async_remote_copy(
            src_ref=source,
            dst_ref=target,
            send_sem=sends.at[number],
            recv_sem=receives.at[number],
            device_id=device,
            device_id_type=MESH,
        )


    raw = key_ref[...].astype(F32)
    scale = lax.rsqrt(jnp.mean(raw * raw, axis=1, keepdims=True) + EPS)
    shards[me, HEAD_ROWS:, 0:DH] = (raw * scale * key_gain_ref[...]).astype(BF16)
    shards[me, HEAD_ROWS:, DH:] = value_ref[...]
    logit = logit_ref[...].astype(F32)
    decay = jnp.minimum(logit, 0.0) - jnp.log1p(jnp.exp(-jnp.abs(logit)))
    row = lax.broadcasted_iota(jnp.int32, (TOK, TOK), 0)
    col = lax.broadcasted_iota(jnp.int32, (TOK, TOK), 1)
    upper = (row <= col).astype(F32)
    local = jnp.dot(decay, upper, preferred_element_type=F32, precision=lax.Precision.HIGHEST)
    local = local * LOG2E
    high = local.astype(BF16).astype(F32)
    mid = (local - high).astype(BF16).astype(F32)
    packed = [high, mid, local - high - mid, jnp.zeros((4, TOK), F32)]
    shards[me, 0:HEAD_ROWS, :] = jnp.concatenate(packed, axis=0).astype(BF16)

    ids = {}
    for tree in (0, 1):
        for name in ring_events():
            ids[tree, name] = len(ids)
    rings = len(ids)


    sent = []

    def send(event, tree, da, db, part, target):
        place = shards.at[shard_at(tree, da, db), rows_of(tree, part)]
        device = device_at(tree, *target)
        remote(place, place, out_send, out_recv, ids[event], device).start()
        sent.append((ids[event], tree, part))

    def share(tree, da, db):
        place = shards.at[shard_at(tree, da, db), rows_of(tree, "ab")]
        number = rings + 2 * step_of(tree, da, db) + tree
        remote(place, place, out_send, out_recv, number, sibling).start()
        sent.append((number, tree, "ab"))

    def wait(tree, name, da, db, part):
        place = shards.at[shard_at(tree, da, db), rows_of(tree, part)]
        remote(place, place, out_send, out_recv, ids[tree, name], sibling).wait_recv()

    for tree in (0, 1):
        send((tree, "A-"), tree, 0, 0, "ab", (1, 0))
        send((tree, "A+"), tree, 0, 0, "ab", (-1, 0))

    line = z * 2 + core
    chunk_sum[y, line] = jnp.concatenate(
        [jnp.broadcast_to(local[:, TOK - 1 :], (4, DH)), jnp.zeros((4, DH), F32)], axis=0
    )

    def sum_copies(axis):
        if axis == 0:
            place, devices = chunk_sum.at[y, line], partners[0]
        else:
            place = chunk_sum.at[y]
            devices = [(z * 8 + ys[step] * 2 + core, rep) for step in (1, 2, 3)]
        return [
            remote(place, place, sum_send, sum_recv, 7 * axis + i, device)
            for i, device in enumerate(devices)
        ]

    def sum_wait(axis):
        for i in range(3 if axis else 7):
            if axis == 0:
                dz, dc = line_steps[i]
                place = chunk_sum.at[y, zs[-dz] * 2 + (other if dc else core)]
            else:
                place = chunk_sum.at[ys[-i - 1]]
            remote(place, place, sum_send, sum_recv, 7 * axis + i, sibling).wait_recv()

    for made in sum_copies(0):
        made.start()
    for tree in (0, 1):
        send((tree, ("B-", 0)), tree, 0, 0, "ab", (0, 1))
        send((tree, ("B+", 0)), tree, 0, 0, "ab", (0, -1))
        share(tree, 0, 0)

    def axis_near():
        for tree in (0, 1):
            wait(tree, "A-", -1, 0, "ab")
            send((tree, "A2a"), tree, -1, 0, "a", (1, 0))
            wait(tree, "A+", 1, 0, "ab")
            send((tree, "A2b"), tree, 1, 0, "b", (-1, 0))
            for da in (-1, 1):
                send((tree, ("B-", da)), tree, da, 0, "ab", (0, 1))
                send((tree, ("B+", da)), tree, da, 0, "ab", (0, -1))
                share(tree, da, 0)

    def axis_far():
        for tree in (0, 1):
            wait(tree, "A2a", 2, 0, "a")
            wait(tree, "A2b", 2, 0, "b")
            send((tree, ("B-", 2)), tree, 2, 0, "ab", (0, 1))
            send((tree, ("B+", 2)), tree, 2, 0, "ab", (0, -1))
            share(tree, 2, 0)

    def near(da):
        for tree in (0, 1):
            wait(tree, ("B-", da), da, -1, "ab")
            send((tree, ("B2a", da)), tree, da, -1, "a", (0, 1))
            wait(tree, ("B+", da), da, 1, "ab")
            send((tree, ("B2b", da)), tree, da, 1, "b", (0, -1))
            share(tree, da, -1)
            share(tree, da, 1)

    def far(da):
        for tree in (0, 1):
            wait(tree, ("B2a", da), da, 2, "a")
            wait(tree, ("B2b", da), da, 2, "b")
            share(tree, da, 2)

    def cross():
        near(1)
        far(0)

    gather_steps = {
        2: axis_far,
        4: functools.partial(near, -1),
        5: cross,
        7: functools.partial(near, 2),
        9: functools.partial(far, -1),
        11: functools.partial(far, 1),
        13: functools.partial(far, 2),
    }


    ones = jnp.ones((TOK, DH), BF16)
    starts = []
    for tile in range(TOK // TILE):
        at = me * (TOK // TILE) + tile
        end = jnp.int32(0)
        start = jnp.int32(0)
        for document in range(4):
            end = end + length_ref[document]
            start = jnp.where(end <= at, end, start)
        starts.append(start * TILE)
    query_scale = query_gain_ref[...] * (DH**-0.5)
    for head in range(HEADS):
        raw = query_ref[:, head * DH : (head + 1) * DH].astype(F32)
        scale = lax.rsqrt(jnp.mean(raw * raw, axis=1, keepdims=True) + EPS)
        normed = (raw * scale * (query_scale * LOG2E)).astype(BF16)
        own_gate = row_to_columns(local[head : head + 1, :])
        query_turned[:, head * TOK : (head + 1) * TOK] = turn(normed.astype(F32)).astype(BF16)
        query_wide[head] = jnp.concatenate([normed, split_lanes(own_gate)], axis=1)
    out_sum[...] = jnp.zeros_like(out_sum)
    offset[...] = jnp.zeros_like(offset)
    lane_token = lax.broadcasted_iota(jnp.int32, (1, TOK), 1)

    def forward_block(block, diagonal):
        keys = shards[block, HEAD_ROWS:, 0:DH]
        values = shards[block, HEAD_ROWS:, DH:]
        key_wide = jnp.concatenate([keys, ones], axis=1)
        value_wide = jnp.concatenate([values, ones], axis=1)
        token = block * TOK + lane_token
        packed = shards[block, 0:HEAD_ROWS, :].astype(F32)
        gate = packed[0:4] + packed[4:8] + packed[8:12]
        if not diagonal:
            before = base[block, 0:4, :]
            gate = gate + jnp.concatenate([before, before], axis=1)
        following = contract_last(query_wide[0], key_wide)
        for head in range(HEADS):
            scores = following
            if head + 1 < HEADS:
                following = contract_last(query_wide[head + 1], key_wide)
            pieces = []
            for tile in range(TOK // TILE):
                low = jnp.where(token >= starts[tile], gate[head : head + 1], jnp.inf)
                pieces.append(scores[tile * TILE : (tile + 1) * TILE] - low)
            scores = jnp.concatenate(pieces, axis=0)
            if diagonal:
                row = lax.broadcasted_iota(jnp.int32, (TOK, TOK), 0)
                col = lax.broadcasted_iota(jnp.int32, (TOK, TOK), 1)
                scores = jnp.where(col <= row, scores, -jnp.inf)
            weights = jnp.exp2(scores).astype(BF16)
            prob[me - block, head * TOK : (head + 1) * TOK, :] = weights
            out_sum[head] += jnp.dot(weights, value_wide, preferred_element_type=F32)

    forward_block(me, True)
    sum_wait(0)
    for made in sum_copies(1):
        made.start()
    axis_near()
    near(0)
    sum_wait(1)

    carry = jnp.zeros((8, DH), F32)
    for shard in range(SHARDS - 1, -1, -1):
        chunk = chunk_sum[(shard // 2) % 4, (shard // 8) * 2 + shard % 2]
        carry = carry - jnp.where(shard < me, chunk, 0.0)
        base[shard] = carry

    def chip_of(step, order):
        return pick(step, [cells[entry] for entry in order])

    def forward_step(step, _):
        cell = chip_of(step, FORWARD)

        for at, action in gather_steps.items():
            pl.when(step == at)(action)

        def one(which, _):
            block = cell * 2 + jnp.where(which == 0, core, 1 - core)

            @pl.when(which == 1)
            def _():
                for tree in (0, 1):
                    place = shards.at[block, rows_of(tree, "ab")]
                    number = rings + 2 * step + tree
                    remote(place, place, out_send, out_recv, number, sibling).wait_recv()

            @pl.when((block < me) & (block >= me - BACK))
            def _():
                forward_block(block, False)

            return 0

        return lax.fori_loop(0, 2, one, 0)

    lax.fori_loop(0, STEPS, forward_step, 0)

    for head in range(HEADS):
        span = slice(head * DH, (head + 1) * DH)
        inverse = 1.0 / out_sum[head, :, DH:]
        out = out_sum[head, :, 0:DH] * inverse
        att_ref[:, span] = out.astype(BF16)
        scaled = (grad_ref[:, span].astype(F32) * inverse).astype(BF16)
        inner = jnp.sum(scaled.astype(F32) * out, axis=1, keepdims=True)
        grad_turned[:, head * TOK : (head + 1) * TOK] = turn(scaled.astype(F32)).astype(BF16)
        grad_wide[head] = jnp.concatenate(
            [scaled, split_lanes(jnp.broadcast_to(-inner, (TOK, DH)))], axis=1
        )
    out_sum[...] = jnp.zeros_like(out_sum)


    back = []

    def land(tree, name, part):
        first, count = piece(tree, part)
        return landed.at[ids[tree, name], pl.ds(first - piece(tree, "ab")[0], count)]

    def give(event, tree, da, db, part, target):
        source = total.at[cell_at(tree, da, db), rows_of(tree, part)]
        device = device_at(tree, *target)
        goal = land(event[0], event[1], part)
        remote(source, goal, back_send, back_recv, ids[event], device).start()
        back.append((ids[event], event[0], event[1], part))

    def landing(tree, name, part):
        goal = land(tree, name, part)
        remote(goal, goal, back_send, back_recv, ids[tree, name], sibling).wait_recv()
        return goal[...]

    def added(terms):
        return functools.reduce(lambda a, b: a + b, [term.astype(F32) for term in terms])

    def put(tree, da, db, part, terms):
        whole = added(terms)
        if tree == 0 and part in ("a", "ab"):
            gates = whole[0:8] + whole[8:16]
            high = gates.astype(BF16).astype(F32)
            whole = jnp.concatenate([high, gates - high, whole[16:]], axis=0)
        total[cell_at(tree, da, db), rows_of(tree, part), :] = whole.astype(BF16)

    def twins(tree, da, db, part):
        place, rows = cell_at(tree, da, db), rows_of(tree, part)
        return [parts[shard_at(tree, da, db), rows, :], twin[place, rows, :]]

    def reduce_item(tree, da, db):
        if db == 2:
            put(tree, da, 2, "ab", twins(tree, da, 2, "ab"))
            give((tree, ("B2a", da)), tree, da, 2, "a", (0, 1))
            give((tree, ("B2b", da)), tree, da, 2, "b", (0, -1))
        elif db in (1, -1):
            name, close, away = ("B2a", "a", "b") if db == 1 else ("B2b", "b", "a")
            put(tree, da, db, away, twins(tree, da, db, away))
            put(tree, da, db, close, twins(tree, da, db, close) + [landing(tree, (name, da), close)])
            give((tree, ("B-" if db == 1 else "B+", da)), tree, da, db, "ab", (0, db))
        else:
            terms = twins(tree, da, 0, "ab")
            terms += [landing(tree, (name, da), "ab") for name in ("B-", "B+")]
            if da == 0:
                terms += [landing(tree, name, "ab") for name in ("A-", "A+")]
                return added(terms)
            put(tree, da, 0, "ab", terms)
            if da == 2:
                give((tree, "A2a"), tree, 2, 0, "a", (1, 0))
                give((tree, "A2b"), tree, 2, 0, "b", (-1, 0))
            else:
                name, part = ("A2a", "a") if da == 1 else ("A2b", "b")
                mine = total[cell_at(tree, da, 0), rows_of(tree, part), :]
                put(tree, da, 0, part, [mine, landing(tree, name, part)])
                give((tree, "A-" if da == 1 else "A+"), tree, da, 0, "ab", (da, 0))
        return None

    def twin_copy(step, source, cell):
        return remote(parts.at[source], twin.at[cell], back_send, back_recv, rings + step, sibling)

    def reduce_turn(turn):
        at = STEPS - turn
        dz, dy = ORDER[at]
        twin_copy(at, cell_at(0, dz, dy) * 2, cell_at(0, dz, dy)).wait_recv()
        items = [(0, dz, dy), (1, dy, dz)]
        now = [item for item in items if item not in [late for _, late in LATE]]
        now += [late for when, late in LATE if when == turn]
        return [reduce_item(*item) for item in now]


    def backward_block(block):
        keys = shards[block, HEAD_ROWS:, 0:DH]
        values = shards[block, HEAD_ROWS:, DH:]
        key_wide = jnp.concatenate([keys, ones], axis=1)
        value_wide = jnp.concatenate([values, ones], axis=1)
        sums = []
        following = contract_last(grad_wide[0], value_wide)
        for head in range(HEADS):
            span = slice(head * TOK, (head + 1) * TOK)
            prob_grad = following
            if head + 1 < HEADS:
                following = contract_last(grad_wide[head + 1], value_wide)
            score_grad = prob[me - block, span, :].astype(F32) * prob_grad
            low = score_grad.astype(BF16)
            folded = jnp.sum(low.astype(F32).reshape(TOK // 8, 8, TOK), axis=0)
            sums.append(jnp.sum(folded, axis=0, keepdims=True))
            score_low[span, :] = low
            out_sum[head] += jnp.dot(low, key_wide, preferred_element_type=F32)
        key_part = (jnp.dot(query_turned[...], score_low[...], preferred_element_type=F32) * LN2).astype(BF16)
        value_part = jnp.dot(grad_turned[...], prob[me - block], preferred_element_type=F32)
        parts[block, HEAD_ROWS : HEAD_ROWS + DH, :] = key_part
        parts[block, HEAD_ROWS + DH :, :] = value_part.astype(BF16)
        columns = jnp.concatenate(sums + [jnp.zeros((4, TOK), F32)], axis=0)
        high = columns.astype(BF16).astype(F32)
        parts[block, 0:HEAD_ROWS, :] = jnp.concatenate([-high, high - columns], axis=0).astype(BF16)
        lane = lax.broadcasted_iota(jnp.int32, (8, DH), 1)
        whole = jnp.broadcast_to(jnp.sum(columns, axis=1, keepdims=True), (8, DH))
        offset[...] += jnp.where((lane >= block) & (lane < me), whole, 0.0)

    def backward_step(turn, _):
        step = STEPS - 1 - turn
        cell = chip_of(step, ORDER)

        def one(which, _):
            block = cell * 2 + jnp.where(which == 1, core, 1 - core)
            used = (block <= me) & (block >= me - BACK)

            @pl.when(used)
            def _():
                backward_block(block)

            @pl.when(jnp.logical_not(used))
            def _():
                parts[block] = jnp.zeros((ROWS, 2 * DH), BF16)

            @pl.when(which == 0)
            def _():
                twin_copy(step, block, cell).start()

            return 0

        lax.fori_loop(0, 2, one, 0)
        for at in range(1, STEPS):

            @pl.when(turn == at)
            def _():
                reduce_turn(at)

        return 0

    lax.fori_loop(0, STEPS, backward_step, 0)


    query_gain_sum = jnp.zeros((1, DH), F32)
    turned = []
    for head in range(HEADS):
        span = slice(head * DH, (head + 1) * DH)
        raw = query_ref[:, span].astype(F32)
        scale = lax.rsqrt(jnp.mean(raw * raw, axis=1, keepdims=True) + EPS)
        hat = raw * scale
        cotangent = out_sum[head, :, 0:DH]
        query_gain_sum += jnp.sum(cotangent * hat, axis=0, keepdims=True)
        inner = cotangent * query_scale
        mean = jnp.mean(inner * hat, axis=1, keepdims=True)
        query_grad_ref[:, span] = (scale * (inner - hat * mean)).astype(BF16)
        halves = [jnp.transpose(out_sum[head, half * DH : (half + 1) * DH, DH:])[0:1] for half in (0, 1)]
        turned.append(jnp.concatenate(halves, axis=1))
    row_sums = jnp.concatenate(turned, axis=0)
    query_gain_sum = query_gain_sum * (DH**-0.5)
    key_gain_row = query_gain_sum * query_gain_ref[...] / key_gain_ref[...]
    small[0] = jnp.concatenate(
        [query_gain_sum, key_gain_row, jnp.zeros((6, DH), F32), offset[...]], axis=0
    )

    def small_copies(axis):
        return [
            remote(small.at[axis], small_landed.at[7 * axis + i], small_send, small_recv, 7 * axis + i, device)
            for i, device in enumerate(partners[axis])
        ]

    def small_add(axis):
        whole = small[axis]
        shared = lax.broadcasted_iota(jnp.int32, (16, DH), 0) < 8
        for i, made in enumerate(small_copies(axis)):
            made.wait_recv()
            term = small_landed[7 * axis + i]
            if axis == 1 and field_steps[i][1]:
                term = jnp.where(shared, term, 0.0)
            whole = whole + term
        small[axis + 1] = whole

    for made in small_copies(0):
        made.start()
    finals = reduce_turn(STEPS)
    small_add(0)
    for made in small_copies(1):
        made.start()

    value_grad_ref[...] = turn(finals[1]).astype(BF16)
    cotangent = turn(finals[0][HEAD_ROWS:])
    raw = key_ref[...].astype(F32)
    scale = lax.rsqrt(jnp.mean(raw * raw, axis=1, keepdims=True) + EPS)
    hat = raw * scale
    inner = cotangent * key_gain_ref[...]
    mean = jnp.mean(inner * hat, axis=1, keepdims=True)
    key_grad_ref[...] = (scale * (inner - hat * mean)).astype(BF16)

    gates = finals[0][0:4] + finals[0][8:12] + row_sums
    row = lax.broadcasted_iota(jnp.int32, (TOK, TOK), 0)
    col = lax.broadcasted_iota(jnp.int32, (TOK, TOK), 1)
    lower = (row >= col).astype(F32)
    suffix = jnp.dot(gates, lower, preferred_element_type=F32, precision=lax.Precision.HIGHEST)
    logit = logit_ref[...].astype(F32)
    small_add(1)
    lane = lax.broadcasted_iota(jnp.int32, (4, DH), 1)
    later = jnp.sum(jnp.where(lane == me, small[2, 8:12, :], 0.0), axis=1, keepdims=True)
    forget_grad_ref[...] = (suffix + later) / (1.0 + jnp.exp(logit))
    gain_out_ref[...] = small[2, 0:2, :]

    for number, tree, part in sent:
        place = shards.at[0, rows_of(tree, part)]
        remote(place, place, out_send, out_recv, number, sibling).wait_send()
    for number, tree, name, part in back:
        goal = land(tree, name, part)
        remote(goal, goal, back_send, back_recv, number, sibling).wait_send()
    for at in range(STEPS):
        twin_copy(at, 0, 0).wait_send()
    for axis in range(2):
        for made in sum_copies(axis) + small_copies(axis):
            made.wait_send()


def fused(lengths_row, key_local, value_local, logit_local, query_local, grad_local, query_gain, key_gain):
    vmem = pl.BlockSpec(memory_space=pltpu.VMEM)
    smem = pl.BlockSpec(memory_space=pltpu.SMEM)
    wide = jax.ShapeDtypeStruct((TOK, HEADS * DH), BF16)
    narrow = jax.ShapeDtypeStruct((TOK, DH), BF16)
    rows = HEADS * TOK
    dma = pltpu.SemaphoreType.DMA
    return pl.pallas_call(
        fused_kernel,
        out_shape=(
            wide,
            wide,
            narrow,
            narrow,
            jax.ShapeDtypeStruct((HEADS, TOK), F32),
            jax.ShapeDtypeStruct((2, DH), F32),
        ),
        in_specs=[smem] + [vmem] * 7,
        out_specs=(vmem,) * 6,
        scratch_shapes=[
            pltpu.VMEM((SHARDS, ROWS, 2 * DH), BF16),
            pltpu.VMEM((4, 8, 8, DH), F32),
            pltpu.VMEM((SHARDS, 8, DH), F32),
            pltpu.VMEM((HEADS, TOK, 2 * DH), BF16),
            pltpu.VMEM((DH, rows), BF16),
            pltpu.VMEM((HEADS, TOK, 2 * DH), BF16),
            pltpu.VMEM((DH, rows), BF16),
            pltpu.VMEM((BACK + 1, rows, TOK), BF16),
            pltpu.VMEM((rows, TOK), BF16),
            pltpu.VMEM((HEADS, TOK, 2 * DH), F32),
            pltpu.VMEM((8, DH), F32),
            pltpu.VMEM((SHARDS, ROWS, 2 * DH), BF16),
            pltpu.VMEM((SHARDS // 2, ROWS, 2 * DH), BF16),
            pltpu.VMEM((SHARDS // 2, ROWS, 2 * DH), BF16),
            pltpu.VMEM((40, PIECES[1][1], 2 * DH), BF16),
            pltpu.VMEM((3, 16, DH), F32),
            pltpu.VMEM((22, 16, DH), F32),
            dma((40 + 2 * STEPS,)),
            dma((40 + 2 * STEPS,)),
            dma((40 + STEPS,)),
            dma((40 + STEPS,)),
            dma((10,)),
            dma((10,)),
            dma((22,)),
            dma((22,)),
        ],
        compiler_params=pltpu.CompilerParams(
            collective_id=0, has_side_effects=True, vmem_limit_bytes=56 * 2**20
        ),
        name="attend_whole",
    )(lengths_row, key_local, value_local, logit_local, query_local, grad_local, query_gain, key_gain)


def write_kernel(*refs):
    count = len(refs) // 2
    for i in range(count):
        refs[count + i][...] = refs[i][...]


def write(*arrays):
    vmem = pl.BlockSpec(memory_space=pltpu.VMEM)
    return pl.pallas_call(
        write_kernel,
        out_shape=tuple(jax.ShapeDtypeStruct(a.shape, a.dtype) for a in arrays),
        in_specs=[vmem] * len(arrays),
        out_specs=(vmem,) * len(arrays),
        name="write_results",
    )(*arrays)


def on_device(queries, key_vectors, values, forget_logit, out_grad, query_gain, key_gain, lengths):
    results = fused(
        lengths[0],
        key_vectors[0],
        values[0],
        forget_logit[0],
        queries[0],
        out_grad[0],
        query_gain.reshape(1, DH),
        key_gain.reshape(1, DH),
    )
    attention, query_grad, key_grad, value_grad, forget_grad, gain_grad = write(*results)
    return (
        attention[None],
        query_grad[None],
        key_grad[None],
        value_grad[None],
        forget_grad[None],
        gain_grad,
    )


def solution(mesh):
    return jax.shard_map(
        on_device,
        mesh=mesh,
        in_specs=(
            P("rep", "seq", None),
            P("rep", "seq", None),
            P("rep", "seq", None),
            P("rep", None, "seq"),
            P("rep", "seq", None),
            P(),
            P(),
            P("rep", None),
        ),
        out_specs=(
            P("rep", "seq", None),
            P("rep", "seq", None),
            P("rep", "seq", None),
            P("rep", "seq", None),
            P("rep", None, "seq"),
            P(),
        ),
        check_vma=False,
    )
```

```python
import functools
import math

import jax
import jax.numpy as jnp
from jax import lax
from jax.experimental import pallas as pl
from jax.experimental.pallas import tpu as pltpu
from jax.sharding import PartitionSpec as P

MESH = pl.DeviceIdType.MESH
F32 = jnp.float32
BF16 = jnp.bfloat16

EPS = 1e-06
HEADS = 4
DH = 128
TOK = 256
TILE = 64
SHARDS = 32
HEAD_ROWS = 16
ROWS = HEAD_ROWS + TOK
PIECES = ((0, 80), (80, 144), (144, 208), (208, 272))
LOG2E = math.log2(math.e)
LN2 = math.log(2.0)
FAR = (2, -1, 1, 0)
BACK = 24
FORWARD = (
    (0, 0), (-1, 0), (0, -1), (1, 0), (0, 1), (2, 0), (0, 2), (-1, -1),
    (-1, 1), (1, -1), (1, 1), (2, -1), (-1, 2), (2, 1), (1, 2), (2, 2),
)
HELD = 5
ORDER = (
    (0, 0), (-1, 0), (0, -1), (1, 0), (0, 1), (-1, -1), (-1, 1), (1, -1),
    (1, 1), (2, 0), (0, 2), (2, -1), (-1, 2), (2, 1), (1, 2), (2, 2),
)
STEPS = len(ORDER)
LATE = (
    (4, (1, 2, 1)), (4, (0, 2, 1)), (5, (1, 2, -1)), (6, (0, 2, -1)), (9, (1, 2, 0)), (9, (0, 2, 0)),
)


def piece(tree, part):
    low, high = PIECES[2 * tree], PIECES[2 * tree + 1]
    first, last = {"a": low, "b": high, "ab": (low[0], high[1])}[part]
    return first, last - first


def rows_of(tree, part):
    first, count = piece(tree, part)
    return pl.ds(first, count)


def greet(devices):
    barrier = pltpu.get_barrier_semaphore()
    for device in devices:
        pl.semaphore_signal(barrier, inc=1, device_id=device, device_id_type=MESH)
    pl.semaphore_wait(barrier, len(devices))


def ring_events():
    names = ["A-", "A+", "A2a", "A2b"]
    for da in FAR:
        names += [("B-", da), ("B+", da), ("B2a", da), ("B2b", da)]
    return names


def split3(x):
    high = x.astype(BF16)
    rest = x - high.astype(F32)
    mid = rest.astype(BF16)
    low = (rest - mid.astype(F32)).astype(BF16)
    return high, mid, low


def row_to_columns(row):
    parts = [
        jnp.transpose(jnp.broadcast_to(row[:, half * DH : (half + 1) * DH], (DH, DH)))
        for half in (0, 1)
    ]
    return jnp.concatenate(parts, axis=0)


def turn(x):
    if x.shape[0] == DH:
        return jnp.concatenate([jnp.transpose(x[:, :DH]), jnp.transpose(x[:, DH:])], axis=0)
    return jnp.concatenate([jnp.transpose(x[:DH]), jnp.transpose(x[DH:])], axis=1)


def split_lanes(full):
    high, mid, low = split3(full)
    lane = lax.broadcasted_iota(jnp.int32, full.shape, 1)
    picked = jnp.where(
        lane == 0,
        high.astype(F32),
        jnp.where(lane == 1, mid.astype(F32), jnp.where(lane == 2, low.astype(F32), 0.0)),
    )
    return picked.astype(BF16)


def contract_last(left, right):
    return lax.dot_general(left, right, (((1,), (1,)), ((), ())), preferred_element_type=F32)


def pick(step, entries):
    found = entries[0]
    for i, entry in enumerate(entries):
        if i:
            found = jnp.where(step == i, entry, found)
    return found


def step_of(tree, da, db):
    return FORWARD.index((da, db) if tree == 0 else (db, da))


def fused_kernel(
    length_ref,
    key_ref,
    value_ref,
    logit_ref,
    query_ref,
    grad_ref,
    query_gain_ref,
    key_gain_ref,
    att_ref,
    query_grad_ref,
    key_grad_ref,
    value_grad_ref,
    forget_grad_ref,
    gain_out_ref,
    shards,
    chunk_sum,
    base,
    query_wide,
    query_turned,
    grad_wide,
    grad_turned,
    prob,
    score_low,
    out_sum,
    offset,
    row_sums,
    parts,
    twin,
    total,
    landed,
    small,
    small_landed,
    out_send,
    out_recv,
    back_send,
    back_recv,
    sum_send,
    sum_recv,
    small_send,
    small_recv,
):
    me, rep = lax.axis_index("seq"), lax.axis_index("rep")
    z, y, core = me // 8, (me // 2) % 4, me % 2
    zs, ys, reps = (
        {step: at if step == 0 else (at + (step + 4) % 4) % 4 for step in range(-3, 4)} for at in (z, y, rep)
    )
    cells = {(dz, dy): zs[dz] * 4 + ys[dy] for dz in FAR for dy in FAR}
    places = {key: cell * 2 + core for key, cell in cells.items()}
    other = 1 - core

    def cell_at(tree, da, db):
        return cells[(da, db) if tree == 0 else (db, da)]

    def shard_at(tree, da, db):
        return places[(da, db) if tree == 0 else (db, da)]

    def device_at(tree, da, db):
        return (shard_at(tree, da, db), rep)

    sibling = (z * 8 + y * 2 + other, rep)
    line_steps = [(dz, dc) for dz in range(4) for dc in range(2) if dz or dc]
    field_steps = [(dy, dx) for dy in range(4) for dx in range(4) if dy or dx]
    partners = [
        [(zs[dz] * 8 + y * 2 + (other if dc else core), rep) for dz, dc in line_steps],
        [(z * 8 + ys[dy] * 2 + core, reps[dx]) for dy, dx in field_steps],
    ]
    greet([device for group in partners for device in group])

    def remote(source, target, sends, receives, number, device):
        return pltpu.make_async_remote_copy(
            src_ref=source,
            dst_ref=target,
            send_sem=sends.at[number],
            recv_sem=receives.at[number],
            device_id=device,
            device_id_type=MESH,
        )


    raw = key_ref[...].astype(F32)
    scale = lax.rsqrt(jnp.mean(raw * raw, axis=1, keepdims=True) + EPS)
    shards[me, HEAD_ROWS:, 0:DH] = (raw * scale * key_gain_ref[...]).astype(BF16)
    shards[me, HEAD_ROWS:, DH:] = value_ref[...]
    logit = logit_ref[...].astype(F32)
    decay = jnp.minimum(logit, 0.0) - jnp.log1p(jnp.exp(-jnp.abs(logit)))
    row = lax.broadcasted_iota(jnp.int32, (TOK, TOK), 0)
    col = lax.broadcasted_iota(jnp.int32, (TOK, TOK), 1)
    upper = (row <= col).astype(F32)
    local = jnp.dot(decay, upper, preferred_element_type=F32, precision=lax.Precision.HIGHEST)
    local = local * LOG2E
    high = local.astype(BF16).astype(F32)
    mid = (local - high).astype(BF16).astype(F32)
    packed = [high, mid, local - high - mid, jnp.zeros((4, TOK), F32)]
    shards[me, 0:HEAD_ROWS, :] = jnp.concatenate(packed, axis=0).astype(BF16)

    ids = {}
    for tree in (0, 1):
        for name in ring_events():
            ids[tree, name] = len(ids)
    rings = len(ids)


    sent = []

    def send(event, tree, da, db, part, target):
        place = shards.at[shard_at(tree, da, db), rows_of(tree, part)]
        device = device_at(tree, *target)
        remote(place, place, out_send, out_recv, ids[event], device).start()
        sent.append((ids[event], tree, part))

    def share(tree, da, db):
        place = shards.at[shard_at(tree, da, db), rows_of(tree, "ab")]
        number = rings + 2 * step_of(tree, da, db) + tree
        remote(place, place, out_send, out_recv, number, sibling).start()
        sent.append((number, tree, "ab"))

    def wait(tree, name, da, db, part):
        place = shards.at[shard_at(tree, da, db), rows_of(tree, part)]
        remote(place, place, out_send, out_recv, ids[tree, name], sibling).wait_recv()

    for tree in (0, 1):
        send((tree, "A-"), tree, 0, 0, "ab", (1, 0))
        send((tree, "A+"), tree, 0, 0, "ab", (-1, 0))

    line = z * 2 + core
    chunk_sum[y, line] = jnp.concatenate(
        [jnp.broadcast_to(local[:, TOK - 1 :], (4, DH)), jnp.zeros((4, DH), F32)], axis=0
    )

    def sum_copies(axis):
        if axis == 0:
            place, devices = chunk_sum.at[y, line], partners[0]
        else:
            place = chunk_sum.at[y]
            devices = [(z * 8 + ys[step] * 2 + core, rep) for step in (1, 2, 3)]
        return [
            remote(place, place, sum_send, sum_recv, 7 * axis + i, device)
            for i, device in enumerate(devices)
        ]

    def sum_wait(axis):
        for i in range(3 if axis else 7):
            if axis == 0:
                dz, dc = line_steps[i]
                place = chunk_sum.at[y, zs[-dz] * 2 + (other if dc else core)]
            else:
                place = chunk_sum.at[ys[-i - 1]]
            remote(place, place, sum_send, sum_recv, 7 * axis + i, sibling).wait_recv()

    for made in sum_copies(0):
        made.start()
    for tree in (0, 1):
        send((tree, ("B-", 0)), tree, 0, 0, "ab", (0, 1))
        send((tree, ("B+", 0)), tree, 0, 0, "ab", (0, -1))
        share(tree, 0, 0)

    def axis_near():
        for tree in (0, 1):
            wait(tree, "A-", -1, 0, "ab")
            send((tree, "A2a"), tree, -1, 0, "a", (1, 0))
            wait(tree, "A+", 1, 0, "ab")
            send((tree, "A2b"), tree, 1, 0, "b", (-1, 0))
            for da in (-1, 1):
                send((tree, ("B-", da)), tree, da, 0, "ab", (0, 1))
                send((tree, ("B+", da)), tree, da, 0, "ab", (0, -1))
                share(tree, da, 0)

    def axis_far():
        for tree in (0, 1):
            wait(tree, "A2a", 2, 0, "a")
            wait(tree, "A2b", 2, 0, "b")
            send((tree, ("B-", 2)), tree, 2, 0, "ab", (0, 1))
            send((tree, ("B+", 2)), tree, 2, 0, "ab", (0, -1))
            share(tree, 2, 0)

    def near(da):
        for tree in (0, 1):
            wait(tree, ("B-", da), da, -1, "ab")
            send((tree, ("B2a", da)), tree, da, -1, "a", (0, 1))
            wait(tree, ("B+", da), da, 1, "ab")
            send((tree, ("B2b", da)), tree, da, 1, "b", (0, -1))
            share(tree, da, -1)
            share(tree, da, 1)

    def far(da):
        for tree in (0, 1):
            wait(tree, ("B2a", da), da, 2, "a")
            wait(tree, ("B2b", da), da, 2, "b")
            share(tree, da, 2)

    def cross():
        near(1)
        far(0)

    gather_steps = {
        2: axis_far,
        4: functools.partial(near, -1),
        5: cross,
        7: functools.partial(near, 2),
        9: functools.partial(far, -1),
        11: functools.partial(far, 1),
        13: functools.partial(far, 2),
    }


    ones = jnp.ones((TOK, DH), BF16)
    starts = []
    for tile in range(TOK // TILE):
        at = me * (TOK // TILE) + tile
        end = jnp.int32(0)
        start = jnp.int32(0)
        for document in range(4):
            end = end + length_ref[document]
            start = jnp.where(end <= at, end, start)
        starts.append(start * TILE)
    query_scale = query_gain_ref[...] * (DH**-0.5)
    for head in range(HEADS):
        raw = query_ref[:, head * DH : (head + 1) * DH].astype(F32)
        scale = lax.rsqrt(jnp.mean(raw * raw, axis=1, keepdims=True) + EPS)
        normed = (raw * scale * (query_scale * LOG2E)).astype(BF16)
        own_gate = row_to_columns(local[head : head + 1, :])
        query_turned[:, head * TOK : (head + 1) * TOK] = turn(normed.astype(F32)).astype(BF16)
        query_wide[head] = jnp.concatenate([normed, split_lanes(own_gate)], axis=1)
    out_sum[...] = jnp.zeros_like(out_sum)
    offset[...] = jnp.zeros_like(offset)
    lane_token = lax.broadcasted_iota(jnp.int32, (1, TOK), 1)

    def forward_block(block, diagonal):
        keys = shards[block, HEAD_ROWS:, 0:DH]
        values = shards[block, HEAD_ROWS:, DH:]
        key_wide = jnp.concatenate([keys, ones], axis=1)
        value_wide = jnp.concatenate([values, ones], axis=1)
        token = block * TOK + lane_token
        packed = shards[block, 0:HEAD_ROWS, :].astype(F32)
        gate = packed[0:4] + packed[4:8] + packed[8:12]
        if not diagonal:
            before = base[block, 0:4, :]
            gate = gate + jnp.concatenate([before, before], axis=1)
        following = contract_last(query_wide[0], key_wide)
        for head in range(HEADS):
            scores = following
            if head + 1 < HEADS:
                following = contract_last(query_wide[head + 1], key_wide)
            pieces = []
            for tile in range(TOK // TILE):
                low = jnp.where(token >= starts[tile], gate[head : head + 1], jnp.inf)
                pieces.append(scores[tile * TILE : (tile + 1) * TILE] - low)
            scores = jnp.concatenate(pieces, axis=0)
            if diagonal:
                row = lax.broadcasted_iota(jnp.int32, (TOK, TOK), 0)
                col = lax.broadcasted_iota(jnp.int32, (TOK, TOK), 1)
                scores = jnp.where(col <= row, scores, -jnp.inf)
            weights = jnp.exp2(scores).astype(BF16)
            prob[me - block, head * TOK : (head + 1) * TOK, :] = weights
            out_sum[head] += jnp.dot(weights, value_wide, preferred_element_type=F32)

    forward_block(me, True)
    sum_wait(0)
    for made in sum_copies(1):
        made.start()
    axis_near()
    near(0)
    sum_wait(1)

    carry = jnp.zeros((8, DH), F32)
    for shard in range(SHARDS - 1, -1, -1):
        chunk = chunk_sum[(shard // 2) % 4, (shard // 8) * 2 + shard % 2]
        carry = carry - jnp.where(shard < me, chunk, 0.0)
        base[shard] = carry

    def chip_of(step, order):
        return pick(step, [cells[entry] for entry in order])

    def forward_step(step, _):
        cell = chip_of(step, FORWARD)

        for at, action in gather_steps.items():
            pl.when(step == at)(action)

        def one(which, _):
            block = cell * 2 + jnp.where(which == 0, core, 1 - core)

            @pl.when(which == 1)
            def _():
                for tree in (0, 1):
                    place = shards.at[block, rows_of(tree, "ab")]
                    number = rings + 2 * step + tree
                    remote(place, place, out_send, out_recv, number, sibling).wait_recv()

            @pl.when((block < me) & (block >= me - BACK))
            def _():
                forward_block(block, False)

            return 0

        return lax.fori_loop(0, 2, one, 0)

    lax.fori_loop(0, STEPS, forward_step, 0)

    for head in range(HEADS):
        span = slice(head * DH, (head + 1) * DH)
        inverse = 1.0 / out_sum[head, :, DH:]
        out = out_sum[head, :, 0:DH] * inverse
        att_ref[:, span] = out.astype(BF16)
        scaled = (grad_ref[:, span].astype(F32) * inverse).astype(BF16)
        inner = jnp.sum(scaled.astype(F32) * out, axis=1, keepdims=True)
        grad_turned[:, head * TOK : (head + 1) * TOK] = turn(scaled.astype(F32)).astype(BF16)
        grad_wide[head] = jnp.concatenate(
            [scaled, split_lanes(jnp.broadcast_to(-inner, (TOK, DH)))], axis=1
        )
    out_sum[...] = jnp.zeros_like(out_sum)


    back = []

    def land(tree, name, part):
        first, count = piece(tree, part)
        return landed.at[ids[tree, name], pl.ds(first - piece(tree, "ab")[0], count)]

    def give(event, tree, da, db, part, target):
        source = total.at[cell_at(tree, da, db), rows_of(tree, part)]
        device = device_at(tree, *target)
        goal = land(event[0], event[1], part)
        remote(source, goal, back_send, back_recv, ids[event], device).start()
        back.append((ids[event], event[0], event[1], part))

    def landing(tree, name, part):
        goal = land(tree, name, part)
        remote(goal, goal, back_send, back_recv, ids[tree, name], sibling).wait_recv()
        return goal[...]

    def added(terms):
        return functools.reduce(lambda a, b: a + b, [term.astype(F32) for term in terms])

    def put(tree, da, db, part, terms):
        whole = added(terms)
        if tree == 0 and part in ("a", "ab"):
            gates = whole[0:8] + whole[8:16]
            high = gates.astype(BF16).astype(F32)
            whole = jnp.concatenate([high, gates - high, whole[16:]], axis=0)
        total[cell_at(tree, da, db), rows_of(tree, part), :] = whole.astype(BF16)

    def twins(tree, da, db, part):
        place, rows = cell_at(tree, da, db), rows_of(tree, part)
        return [parts[shard_at(tree, da, db), rows, :], twin[place, rows, :]]

    def reduce_item(tree, da, db):
        if db == 2:
            put(tree, da, 2, "ab", twins(tree, da, 2, "ab"))
            give((tree, ("B2a", da)), tree, da, 2, "a", (0, 1))
            give((tree, ("B2b", da)), tree, da, 2, "b", (0, -1))
        elif db in (1, -1):
            name, close, away = ("B2a", "a", "b") if db == 1 else ("B2b", "b", "a")
            put(tree, da, db, away, twins(tree, da, db, away))
            put(tree, da, db, close, twins(tree, da, db, close) + [landing(tree, (name, da), close)])
            give((tree, ("B-" if db == 1 else "B+", da)), tree, da, db, "ab", (0, db))
        else:
            terms = twins(tree, da, 0, "ab")
            terms += [landing(tree, (name, da), "ab") for name in ("B-", "B+")]
            if da == 0:
                terms += [landing(tree, name, "ab") for name in ("A-", "A+")]
                return added(terms)
            put(tree, da, 0, "ab", terms)
            if da == 2:
                give((tree, "A2a"), tree, 2, 0, "a", (1, 0))
                give((tree, "A2b"), tree, 2, 0, "b", (-1, 0))
            else:
                name, part = ("A2a", "a") if da == 1 else ("A2b", "b")
                mine = total[cell_at(tree, da, 0), rows_of(tree, part), :]
                put(tree, da, 0, part, [mine, landing(tree, name, part)])
                give((tree, "A-" if da == 1 else "A+"), tree, da, 0, "ab", (da, 0))
        return None

    def twin_copy(step, source, cell):
        return remote(parts.at[source], twin.at[cell], back_send, back_recv, rings + step, sibling)

    def reduce_turn(turn):
        at = STEPS - turn
        dz, dy = ORDER[at]
        twin_copy(at, cell_at(0, dz, dy) * 2, cell_at(0, dz, dy)).wait_recv()
        items = [(0, dz, dy), (1, dy, dz)]
        now = [item for item in items if item not in [late for _, late in LATE]]
        now += [late for when, late in LATE if when == turn]
        return [reduce_item(*item) for item in now]


    def score_block(block, slot):
        keys = shards[block, HEAD_ROWS:, 0:DH]
        values = shards[block, HEAD_ROWS:, DH:]
        key_wide = jnp.concatenate([keys, ones], axis=1)
        value_wide = jnp.concatenate([values, ones], axis=1)
        sums = []
        following = contract_last(grad_wide[0], value_wide)
        for head in range(HEADS):
            span = slice(head * TOK, (head + 1) * TOK)
            prob_grad = following
            if head + 1 < HEADS:
                following = contract_last(grad_wide[head + 1], value_wide)
            score_grad = prob[me - block, span, :].astype(F32) * prob_grad
            low = score_grad.astype(BF16)
            folded = jnp.sum(low.astype(F32).reshape(TOK // 8, 8, TOK), axis=0)
            sums.append(jnp.sum(folded, axis=0, keepdims=True))
            score_low[slot, span, :] = low
            out_sum[head] += jnp.dot(low, key_wide, preferred_element_type=F32)
        columns = jnp.concatenate(sums + [jnp.zeros((4, TOK), F32)], axis=0)
        high = columns.astype(BF16).astype(F32)
        parts[block, 0:HEAD_ROWS, :] = jnp.concatenate([-high, high - columns], axis=0).astype(BF16)
        lane = lax.broadcasted_iota(jnp.int32, (8, DH), 1)
        whole = jnp.broadcast_to(jnp.sum(columns, axis=1, keepdims=True), (8, DH))
        offset[...] += jnp.where((lane >= block) & (lane < me), whole, 0.0)

    def product_block(block, slot):
        key_part = jnp.dot(query_turned[...], score_low[slot], preferred_element_type=F32) * LN2
        value_part = jnp.dot(grad_turned[...], prob[me - block], preferred_element_type=F32)
        parts[block, HEAD_ROWS : HEAD_ROWS + DH, :] = key_part.astype(BF16)
        parts[block, HEAD_ROWS + DH :, :] = value_part.astype(BF16)

    def block_of(cell, which):
        block = cell * 2 + jnp.where(which == 1, core, 1 - core)
        return block, (block <= me) & (block >= me - BACK)

    def small_copies(axis):
        return [
            remote(small.at[axis], small_landed.at[7 * axis + i], small_send, small_recv, 7 * axis + i, device)
            for i, device in enumerate(partners[axis])
        ]

    def small_add(axis):
        whole = small[axis]
        shared = lax.broadcasted_iota(jnp.int32, (16, DH), 0) < 8
        for i, made in enumerate(small_copies(axis)):
            made.wait_recv()
            term = small_landed[7 * axis + i]
            if axis == 1 and field_steps[i][1]:
                term = jnp.where(shared, term, 0.0)
            whole = whole + term
        small[axis + 1] = whole

    def backward_step(held, turn, _):
        step = STEPS - 1 - turn
        cell = chip_of(step, ORDER)

        def one(which, _):
            block, used = block_of(cell, which)
            slot = step * 2 + which if held else 0

            @pl.when(used)
            def _():
                if not held:
                    score_block(block, slot)
                product_block(block, slot)

            @pl.when(jnp.logical_not(used))
            def _():
                parts[block] = jnp.zeros((ROWS, 2 * DH), BF16)

            @pl.when(which == 0)
            def _():
                twin_copy(step, block, cell).start()

            return 0

        lax.fori_loop(0, 2, one, 0)
        first = STEPS - HELD
        for at in range(first + 1, STEPS) if held else range(1, first):

            @pl.when(turn == at)
            def _():
                reduce_turn(at)
                if at == STEPS - 2:
                    small_add(0)
                    for made in small_copies(1):
                        made.start()

        return 0

    def held_step(step, _):
        cell = chip_of(step, ORDER)

        def one(which, _):
            block, used = block_of(cell, which)

            @pl.when(used)
            def _():
                score_block(block, step * 2 + which)

            return 0

        return lax.fori_loop(0, 2, one, 0)

    lax.fori_loop(0, STEPS - HELD, functools.partial(backward_step, False), 0)
    lax.fori_loop(0, HELD, held_step, 0)
    reduce_turn(STEPS - HELD)


    query_gain_sum = jnp.zeros((1, DH), F32)
    turned = []
    for head in range(HEADS):
        span = slice(head * DH, (head + 1) * DH)
        raw = query_ref[:, span].astype(F32)
        scale = lax.rsqrt(jnp.mean(raw * raw, axis=1, keepdims=True) + EPS)
        hat = raw * scale
        cotangent = out_sum[head, :, 0:DH]
        query_gain_sum += jnp.sum(cotangent * hat, axis=0, keepdims=True)
        inner = cotangent * query_scale
        mean = jnp.mean(inner * hat, axis=1, keepdims=True)
        query_grad_ref[:, span] = (scale * (inner - hat * mean)).astype(BF16)
        halves = [jnp.transpose(out_sum[head, half * DH : (half + 1) * DH, DH:])[0:1] for half in (0, 1)]
        turned.append(jnp.concatenate(halves, axis=1))
    row_sums[...] = jnp.concatenate(turned, axis=0)
    query_gain_sum = query_gain_sum * (DH**-0.5)
    key_gain_row = query_gain_sum * query_gain_ref[...] / key_gain_ref[...]
    small[0] = jnp.concatenate(
        [query_gain_sum, key_gain_row, jnp.zeros((6, DH), F32), offset[...]], axis=0
    )

    for made in small_copies(0):
        made.start()
    lax.fori_loop(STEPS - HELD, STEPS, functools.partial(backward_step, True), 0)
    finals = reduce_turn(STEPS)

    value_grad_ref[...] = turn(finals[1]).astype(BF16)
    cotangent = turn(finals[0][HEAD_ROWS:])
    raw = key_ref[...].astype(F32)
    scale = lax.rsqrt(jnp.mean(raw * raw, axis=1, keepdims=True) + EPS)
    hat = raw * scale
    inner = cotangent * key_gain_ref[...]
    mean = jnp.mean(inner * hat, axis=1, keepdims=True)
    key_grad_ref[...] = (scale * (inner - hat * mean)).astype(BF16)

    gates = finals[0][0:4] + finals[0][8:12] + row_sums[...]
    row = lax.broadcasted_iota(jnp.int32, (TOK, TOK), 0)
    col = lax.broadcasted_iota(jnp.int32, (TOK, TOK), 1)
    lower = (row >= col).astype(F32)
    suffix = jnp.dot(gates, lower, preferred_element_type=F32, precision=lax.Precision.HIGHEST)
    logit = logit_ref[...].astype(F32)
    small_add(1)
    lane = lax.broadcasted_iota(jnp.int32, (4, DH), 1)
    later = jnp.sum(jnp.where(lane == me, small[2, 8:12, :], 0.0), axis=1, keepdims=True)
    forget_grad_ref[...] = (suffix + later) / (1.0 + jnp.exp(logit))
    gain_out_ref[...] = small[2, 0:2, :]

    for number, tree, part in sent:
        place = shards.at[0, rows_of(tree, part)]
        remote(place, place, out_send, out_recv, number, sibling).wait_send()
    for number, tree, name, part in back:
        goal = land(tree, name, part)
        remote(goal, goal, back_send, back_recv, number, sibling).wait_send()
    for at in range(STEPS):
        twin_copy(at, 0, 0).wait_send()
    for axis in range(2):
        for made in sum_copies(axis) + small_copies(axis):
            made.wait_send()


def fused(lengths_row, key_local, value_local, logit_local, query_local, grad_local, query_gain, key_gain):
    vmem = pl.BlockSpec(memory_space=pltpu.VMEM)
    smem = pl.BlockSpec(memory_space=pltpu.SMEM)
    wide = jax.ShapeDtypeStruct((TOK, HEADS * DH), BF16)
    narrow = jax.ShapeDtypeStruct((TOK, DH), BF16)
    rows = HEADS * TOK
    dma = pltpu.SemaphoreType.DMA
    return pl.pallas_call(
        fused_kernel,
        out_shape=(
            wide,
            wide,
            narrow,
            narrow,
            jax.ShapeDtypeStruct((HEADS, TOK), F32),
            jax.ShapeDtypeStruct((2, DH), F32),
        ),
        in_specs=[smem] + [vmem] * 7,
        out_specs=(vmem,) * 6,
        scratch_shapes=[
            pltpu.VMEM((SHARDS, ROWS, 2 * DH), BF16),
            pltpu.VMEM((4, 8, 8, DH), F32),
            pltpu.VMEM((SHARDS, 8, DH), F32),
            pltpu.VMEM((HEADS, TOK, 2 * DH), BF16),
            pltpu.VMEM((DH, rows), BF16),
            pltpu.VMEM((HEADS, TOK, 2 * DH), BF16),
            pltpu.VMEM((DH, rows), BF16),
            pltpu.VMEM((BACK + 1, rows, TOK), BF16),
            pltpu.VMEM((2 * HELD, rows, TOK), BF16),
            pltpu.VMEM((HEADS, TOK, 2 * DH), F32),
            pltpu.VMEM((8, DH), F32),
            pltpu.VMEM((HEADS, TOK), F32),
            pltpu.VMEM((SHARDS, ROWS, 2 * DH), BF16),
            pltpu.VMEM((SHARDS // 2, ROWS, 2 * DH), BF16),
            pltpu.VMEM((SHARDS // 2, ROWS, 2 * DH), BF16),
            pltpu.VMEM((40, PIECES[1][1], 2 * DH), BF16),
            pltpu.VMEM((3, 16, DH), F32),
            pltpu.VMEM((22, 16, DH), F32),
            dma((40 + 2 * STEPS,)),
            dma((40 + 2 * STEPS,)),
            dma((40 + STEPS,)),
            dma((40 + STEPS,)),
            dma((10,)),
            dma((10,)),
            dma((22,)),
            dma((22,)),
        ],
        compiler_params=pltpu.CompilerParams(
            collective_id=0, has_side_effects=True, vmem_limit_bytes=56 * 2**20
        ),
        name="attend_whole",
    )(lengths_row, key_local, value_local, logit_local, query_local, grad_local, query_gain, key_gain)


def write_kernel(*refs):
    count = len(refs) // 2
    for i in range(count):
        refs[count + i][...] = refs[i][...]


def write(*arrays):
    vmem = pl.BlockSpec(memory_space=pltpu.VMEM)
    return pl.pallas_call(
        write_kernel,
        out_shape=tuple(jax.ShapeDtypeStruct(a.shape, a.dtype) for a in arrays),
        in_specs=[vmem] * len(arrays),
        out_specs=(vmem,) * len(arrays),
        name="write_results",
    )(*arrays)


def on_device(queries, key_vectors, values, forget_logit, out_grad, query_gain, key_gain, lengths):
    results = fused(
        lengths[0],
        key_vectors[0],
        values[0],
        forget_logit[0],
        queries[0],
        out_grad[0],
        query_gain.reshape(1, DH),
        key_gain.reshape(1, DH),
    )
    attention, query_grad, key_grad, value_grad, forget_grad, gain_grad = write(*results)
    return (
        attention[None],
        query_grad[None],
        key_grad[None],
        value_grad[None],
        forget_grad[None],
        gain_grad,
    )


def solution(mesh):
    return jax.shard_map(
        on_device,
        mesh=mesh,
        in_specs=(
            P("rep", "seq", None),
            P("rep", "seq", None),
            P("rep", "seq", None),
            P("rep", None, "seq"),
            P("rep", "seq", None),
            P(),
            P(),
            P("rep", None),
        ),
        out_specs=(
            P("rep", "seq", None),
            P("rep", "seq", None),
            P("rep", "seq", None),
            P("rep", "seq", None),
            P("rep", None, "seq"),
            P(),
        ),
        check_vma=False,
    )
```

```python
import functools
import math

import jax
import jax.numpy as jnp
from jax import lax
from jax.experimental import pallas as pl
from jax.experimental.pallas import tpu as pltpu
from jax.sharding import PartitionSpec as P

MESH = pl.DeviceIdType.MESH
F32 = jnp.float32
BF16 = jnp.bfloat16

EPS = 1e-06
HEADS = 4
DH = 128
TOK = 256
TILE = 64
SHARDS = 32
HEAD_ROWS = 16
ROWS = HEAD_ROWS + TOK
PIECES = ((0, 80), (80, 144), (144, 208), (208, 272))
LOG2E = math.log2(math.e)
LN2 = math.log(2.0)
FAR = (2, -1, 1, 0)
BACK = 24
FORWARD = (
    (0, 0), (-1, 0), (0, -1), (1, 0), (0, 1), (2, 0), (0, 2), (-1, -1),
    (-1, 1), (1, -1), (1, 1), (2, -1), (-1, 2), (2, 1), (1, 2), (2, 2),
)
HELD = 5
ORDER = (
    (0, 0), (-1, 0), (0, -1), (1, 0), (0, 1), (-1, -1), (-1, 1), (1, -1),
    (1, 1), (2, 0), (0, 2), (2, -1), (-1, 2), (2, 1), (1, 2), (2, 2),
)
STEPS = len(ORDER)
LATE = (
    (4, (1, 2, 1)), (4, (0, 2, 1)), (5, (1, 2, -1)), (6, (0, 2, -1)), (9, (1, 2, 0)), (9, (0, 2, 0)),
)


def piece(tree, part):
    low, high = PIECES[2 * tree], PIECES[2 * tree + 1]
    first, last = {"a": low, "b": high, "ab": (low[0], high[1])}[part]
    return first, last - first


def rows_of(tree, part):
    first, count = piece(tree, part)
    return pl.ds(first, count)


def ring_events():
    names = ["A-", "A+", "A2a", "A2b"]
    for da in FAR:
        names += [("B-", da), ("B+", da), ("B2a", da), ("B2b", da)]
    return names


def split3(x):
    high = x.astype(BF16)
    rest = x - high.astype(F32)
    mid = rest.astype(BF16)
    low = (rest - mid.astype(F32)).astype(BF16)
    return high, mid, low


def row_to_columns(row):
    parts = [
        jnp.transpose(jnp.broadcast_to(row[:, half * DH : (half + 1) * DH], (DH, DH)))
        for half in (0, 1)
    ]
    return jnp.concatenate(parts, axis=0)


def turn(x):
    if x.shape[0] == DH:
        return jnp.concatenate([jnp.transpose(x[:, :DH]), jnp.transpose(x[:, DH:])], axis=0)
    return jnp.concatenate([jnp.transpose(x[:DH]), jnp.transpose(x[DH:])], axis=1)


def split_lanes(full):
    high, mid, low = split3(full)
    lane = lax.broadcasted_iota(jnp.int32, full.shape, 1)
    picked = jnp.where(
        lane == 0,
        high.astype(F32),
        jnp.where(lane == 1, mid.astype(F32), jnp.where(lane == 2, low.astype(F32), 0.0)),
    )
    return picked.astype(BF16)


def contract_last(left, right):
    return lax.dot_general(left, right, (((1,), (1,)), ((), ())), preferred_element_type=F32)


def pick(step, entries):
    found = entries[0]
    for i, entry in enumerate(entries):
        if i:
            found = jnp.where(step == i, entry, found)
    return found


def step_of(tree, da, db):
    return FORWARD.index((da, db) if tree == 0 else (db, da))


def fused_kernel(
    length_ref,
    key_ref,
    value_ref,
    logit_ref,
    query_ref,
    grad_ref,
    query_gain_ref,
    key_gain_ref,
    att_ref,
    query_grad_ref,
    key_grad_ref,
    value_grad_ref,
    forget_grad_ref,
    gain_out_ref,
    shards,
    chunk_sum,
    base,
    query_wide,
    query_turned,
    grad_wide,
    grad_turned,
    prob,
    score_low,
    out_sum,
    offset,
    row_sums,
    parts,
    twin,
    total,
    landed,
    small,
    small_landed,
    out_send,
    out_recv,
    back_send,
    back_recv,
    sum_send,
    sum_recv,
    small_send,
    small_recv,
):
    me, rep = lax.axis_index("seq"), lax.axis_index("rep")
    z, y, core = me // 8, (me // 2) % 4, me % 2
    zs, ys, reps = (
        {step: at if step == 0 else (at + (step + 4) % 4) % 4 for step in range(-3, 4)} for at in (z, y, rep)
    )
    cells = {(dz, dy): zs[dz] * 4 + ys[dy] for dz in FAR for dy in FAR}
    places = {key: cell * 2 + core for key, cell in cells.items()}
    other = 1 - core

    def cell_at(tree, da, db):
        return cells[(da, db) if tree == 0 else (db, da)]

    def shard_at(tree, da, db):
        return places[(da, db) if tree == 0 else (db, da)]

    def device_at(tree, da, db):
        return (shard_at(tree, da, db), rep)

    sibling = (z * 8 + y * 2 + other, rep)
    line_steps = [(dz, dc) for dz in range(4) for dc in range(2) if dz or dc]
    field_steps = [(dy, dx) for dy in range(4) for dx in range(4) if dy or dx]
    partners = [
        [(zs[dz] * 8 + y * 2 + (other if dc else core), rep) for dz, dc in line_steps],
        [(z * 8 + ys[dy] * 2 + core, reps[dx]) for dy, dx in field_steps],
    ]
    met = [device for group in partners for device in group]
    barrier = pltpu.get_barrier_semaphore()
    for device in met:
        pl.semaphore_signal(barrier, inc=1, device_id=device, device_id_type=MESH)

    def remote(source, target, sends, receives, number, device):
        return pltpu.make_async_remote_copy(
            src_ref=source,
            dst_ref=target,
            send_sem=sends.at[number],
            recv_sem=receives.at[number],
            device_id=device,
            device_id_type=MESH,
        )


    raw = key_ref[...].astype(F32)
    scale = lax.rsqrt(jnp.mean(raw * raw, axis=1, keepdims=True) + EPS)
    shards[me, HEAD_ROWS:, 0:DH] = (raw * scale * key_gain_ref[...]).astype(BF16)
    shards[me, HEAD_ROWS:, DH:] = value_ref[...]
    logit = logit_ref[...].astype(F32)
    decay = jnp.minimum(logit, 0.0) - jnp.log1p(jnp.exp(-jnp.abs(logit)))
    row = lax.broadcasted_iota(jnp.int32, (TOK, TOK), 0)
    col = lax.broadcasted_iota(jnp.int32, (TOK, TOK), 1)
    upper = (row <= col).astype(F32)
    local = jnp.dot(decay, upper, preferred_element_type=F32, precision=lax.Precision.HIGHEST)
    local = local * LOG2E
    high = local.astype(BF16).astype(F32)
    mid = (local - high).astype(BF16).astype(F32)
    packed = [high, mid, local - high - mid, jnp.zeros((4, TOK), F32)]
    shards[me, 0:HEAD_ROWS, :] = jnp.concatenate(packed, axis=0).astype(BF16)
    pl.semaphore_wait(barrier, len(met))

    ids = {}
    for tree in (0, 1):
        for name in ring_events():
            ids[tree, name] = len(ids)
    rings = len(ids)


    sent = []

    def send(event, tree, da, db, part, target):
        place = shards.at[shard_at(tree, da, db), rows_of(tree, part)]
        device = device_at(tree, *target)
        remote(place, place, out_send, out_recv, ids[event], device).start()
        sent.append((ids[event], tree, part))

    def share(tree, da, db):
        place = shards.at[shard_at(tree, da, db), rows_of(tree, "ab")]
        number = rings + 2 * step_of(tree, da, db) + tree
        remote(place, place, out_send, out_recv, number, sibling).start()
        sent.append((number, tree, "ab"))

    def wait(tree, name, da, db, part):
        place = shards.at[shard_at(tree, da, db), rows_of(tree, part)]
        remote(place, place, out_send, out_recv, ids[tree, name], sibling).wait_recv()

    line = z * 2 + core
    chunk_sum[y, line] = jnp.concatenate(
        [jnp.broadcast_to(local[:, TOK - 1 :], (4, DH)), jnp.zeros((4, DH), F32)], axis=0
    )

    def sum_copies(axis):
        if axis == 0:
            place, devices = chunk_sum.at[y, line], partners[0]
        else:
            place = chunk_sum.at[y]
            devices = [(z * 8 + ys[step] * 2 + core, rep) for step in (1, 2, 3)]
        return [
            remote(place, place, sum_send, sum_recv, 7 * axis + i, device)
            for i, device in enumerate(devices)
        ]

    def sum_wait(axis):
        for i in range(3 if axis else 7):
            if axis == 0:
                dz, dc = line_steps[i]
                place = chunk_sum.at[y, zs[-dz] * 2 + (other if dc else core)]
            else:
                place = chunk_sum.at[ys[-i - 1]]
            remote(place, place, sum_send, sum_recv, 7 * axis + i, sibling).wait_recv()

    for made in sum_copies(0):
        made.start()
    for tree in (0, 1):
        send((tree, "A-"), tree, 0, 0, "ab", (1, 0))
        send((tree, "A+"), tree, 0, 0, "ab", (-1, 0))

    for tree in (0, 1):
        send((tree, ("B-", 0)), tree, 0, 0, "ab", (0, 1))
        send((tree, ("B+", 0)), tree, 0, 0, "ab", (0, -1))
        share(tree, 0, 0)

    def axis_near():
        for tree in (0, 1):
            wait(tree, "A-", -1, 0, "ab")
            send((tree, "A2a"), tree, -1, 0, "a", (1, 0))
            wait(tree, "A+", 1, 0, "ab")
            send((tree, "A2b"), tree, 1, 0, "b", (-1, 0))
            for da in (-1, 1):
                send((tree, ("B-", da)), tree, da, 0, "ab", (0, 1))
                send((tree, ("B+", da)), tree, da, 0, "ab", (0, -1))
                share(tree, da, 0)

    def axis_far():
        for tree in (0, 1):
            wait(tree, "A2a", 2, 0, "a")
            wait(tree, "A2b", 2, 0, "b")
            send((tree, ("B-", 2)), tree, 2, 0, "ab", (0, 1))
            send((tree, ("B+", 2)), tree, 2, 0, "ab", (0, -1))
            share(tree, 2, 0)

    def near(da):
        for tree in (0, 1):
            wait(tree, ("B-", da), da, -1, "ab")
            send((tree, ("B2a", da)), tree, da, -1, "a", (0, 1))
            wait(tree, ("B+", da), da, 1, "ab")
            send((tree, ("B2b", da)), tree, da, 1, "b", (0, -1))
            share(tree, da, -1)
            share(tree, da, 1)

    def far(da):
        for tree in (0, 1):
            wait(tree, ("B2a", da), da, 2, "a")
            wait(tree, ("B2b", da), da, 2, "b")
            share(tree, da, 2)

    def cross():
        near(1)
        far(0)

    gather_steps = {
        2: axis_far,
        4: functools.partial(near, -1),
        5: cross,
        7: functools.partial(near, 2),
        9: functools.partial(far, -1),
        11: functools.partial(far, 1),
        13: functools.partial(far, 2),
    }


    ones = jnp.ones((TOK, DH), BF16)
    starts = []
    for tile in range(TOK // TILE):
        at = me * (TOK // TILE) + tile
        end = jnp.int32(0)
        start = jnp.int32(0)
        for document in range(4):
            end = end + length_ref[document]
            start = jnp.where(end <= at, end, start)
        starts.append(start * TILE)
    query_scale = query_gain_ref[...] * (DH**-0.5)
    for head in range(HEADS):
        raw = query_ref[:, head * DH : (head + 1) * DH].astype(F32)
        scale = lax.rsqrt(jnp.mean(raw * raw, axis=1, keepdims=True) + EPS)
        normed = (raw * scale * (query_scale * LOG2E)).astype(BF16)
        own_gate = row_to_columns(local[head : head + 1, :])
        query_turned[:, head * TOK : (head + 1) * TOK] = turn(normed.astype(F32)).astype(BF16)
        query_wide[head] = jnp.concatenate([normed, split_lanes(own_gate)], axis=1)
    out_sum[...] = jnp.zeros_like(out_sum)
    offset[...] = jnp.zeros_like(offset)
    lane_token = lax.broadcasted_iota(jnp.int32, (1, TOK), 1)

    def forward_block(block, diagonal):
        keys = shards[block, HEAD_ROWS:, 0:DH]
        values = shards[block, HEAD_ROWS:, DH:]
        key_wide = jnp.concatenate([keys, ones], axis=1)
        value_wide = jnp.concatenate([values, ones], axis=1)
        token = block * TOK + lane_token
        packed = shards[block, 0:HEAD_ROWS, :].astype(F32)
        gate = packed[0:4] + packed[4:8] + packed[8:12]
        if not diagonal:
            before = base[block, 0:4, :]
            gate = gate + jnp.concatenate([before, before], axis=1)
        following = contract_last(query_wide[0], key_wide)
        for head in range(HEADS):
            scores = following
            if head + 1 < HEADS:
                following = contract_last(query_wide[head + 1], key_wide)
            pieces = []
            for tile in range(TOK // TILE):
                low = jnp.where(token >= starts[tile], gate[head : head + 1], jnp.inf)
                pieces.append(scores[tile * TILE : (tile + 1) * TILE] - low)
            scores = jnp.concatenate(pieces, axis=0)
            if diagonal:
                row = lax.broadcasted_iota(jnp.int32, (TOK, TOK), 0)
                col = lax.broadcasted_iota(jnp.int32, (TOK, TOK), 1)
                scores = jnp.where(col <= row, scores, -jnp.inf)
            weights = jnp.exp2(scores).astype(BF16)
            prob[me - block, head * TOK : (head + 1) * TOK, :] = weights
            out_sum[head] += jnp.dot(weights, value_wide, preferred_element_type=F32)

    forward_block(me, True)
    sum_wait(0)
    for made in sum_copies(1):
        made.start()
    axis_near()
    near(0)
    sum_wait(1)

    carry = jnp.zeros((8, DH), F32)
    for shard in range(SHARDS - 1, -1, -1):
        chunk = chunk_sum[(shard // 2) % 4, (shard // 8) * 2 + shard % 2]
        carry = carry - jnp.where(shard < me, chunk, 0.0)
        base[shard] = carry

    def chip_of(step, order):
        return pick(step, [cells[entry] for entry in order])

    def forward_step(step, _):
        cell = chip_of(step, FORWARD)

        for at, action in gather_steps.items():
            pl.when(step == at)(action)

        def one(which, _):
            block = cell * 2 + jnp.where(which == 0, core, 1 - core)

            @pl.when(which == 1)
            def _():
                for tree in (0, 1):
                    place = shards.at[block, rows_of(tree, "ab")]
                    number = rings + 2 * step + tree
                    remote(place, place, out_send, out_recv, number, sibling).wait_recv()

            @pl.when((block < me) & (block >= me - BACK))
            def _():
                forward_block(block, False)

            return 0

        return lax.fori_loop(0, 2, one, 0)

    lax.fori_loop(0, STEPS, forward_step, 0)

    for head in range(HEADS):
        span = slice(head * DH, (head + 1) * DH)
        inverse = 1.0 / out_sum[head, :, DH:]
        out = out_sum[head, :, 0:DH] * inverse
        att_ref[:, span] = out.astype(BF16)
        scaled = (grad_ref[:, span].astype(F32) * inverse).astype(BF16)
        inner = jnp.sum(scaled.astype(F32) * out, axis=1, keepdims=True)
        grad_turned[:, head * TOK : (head + 1) * TOK] = turn(scaled.astype(F32)).astype(BF16)
        grad_wide[head] = jnp.concatenate(
            [scaled, split_lanes(jnp.broadcast_to(-inner, (TOK, DH)))], axis=1
        )
    out_sum[...] = jnp.zeros_like(out_sum)


    back = []

    def land(tree, name, part):
        first, count = piece(tree, part)
        return landed.at[ids[tree, name], pl.ds(first - piece(tree, "ab")[0], count)]

    def give(event, tree, da, db, part, target):
        source = total.at[cell_at(tree, da, db), rows_of(tree, part)]
        device = device_at(tree, *target)
        goal = land(event[0], event[1], part)
        remote(source, goal, back_send, back_recv, ids[event], device).start()
        back.append((ids[event], event[0], event[1], part))

    def landing(tree, name, part):
        goal = land(tree, name, part)
        remote(goal, goal, back_send, back_recv, ids[tree, name], sibling).wait_recv()
        return goal[...]

    def added(terms):
        return functools.reduce(lambda a, b: a + b, [term.astype(F32) for term in terms])

    def put(tree, da, db, part, terms):
        whole = added(terms)
        if tree == 0 and part in ("a", "ab"):
            gates = whole[0:8] + whole[8:16]
            high = gates.astype(BF16).astype(F32)
            whole = jnp.concatenate([high, gates - high, whole[16:]], axis=0)
        total[cell_at(tree, da, db), rows_of(tree, part), :] = whole.astype(BF16)

    def twins(tree, da, db, part):
        place, rows = cell_at(tree, da, db), rows_of(tree, part)
        return [parts[shard_at(tree, da, db), rows, :], twin[place, rows, :]]

    def reduce_item(tree, da, db):
        if db == 2:
            put(tree, da, 2, "ab", twins(tree, da, 2, "ab"))
            give((tree, ("B2a", da)), tree, da, 2, "a", (0, 1))
            give((tree, ("B2b", da)), tree, da, 2, "b", (0, -1))
        elif db in (1, -1):
            name, close, away = ("B2a", "a", "b") if db == 1 else ("B2b", "b", "a")
            put(tree, da, db, away, twins(tree, da, db, away))
            put(tree, da, db, close, twins(tree, da, db, close) + [landing(tree, (name, da), close)])
            give((tree, ("B-" if db == 1 else "B+", da)), tree, da, db, "ab", (0, db))
        else:
            terms = twins(tree, da, 0, "ab")
            terms += [landing(tree, (name, da), "ab") for name in ("B-", "B+")]
            if da == 0:
                terms += [landing(tree, name, "ab") for name in ("A-", "A+")]
                return added(terms)
            put(tree, da, 0, "ab", terms)
            if da == 2:
                give((tree, "A2a"), tree, 2, 0, "a", (1, 0))
                give((tree, "A2b"), tree, 2, 0, "b", (-1, 0))
            else:
                name, part = ("A2a", "a") if da == 1 else ("A2b", "b")
                mine = total[cell_at(tree, da, 0), rows_of(tree, part), :]
                put(tree, da, 0, part, [mine, landing(tree, name, part)])
                give((tree, "A-" if da == 1 else "A+"), tree, da, 0, "ab", (da, 0))
        return None

    def twin_copy(step, source, cell):
        return remote(parts.at[source], twin.at[cell], back_send, back_recv, rings + step, sibling)

    def reduce_turn(turn):
        at = STEPS - turn
        dz, dy = ORDER[at]
        twin_copy(at, cell_at(0, dz, dy) * 2, cell_at(0, dz, dy)).wait_recv()
        items = [(0, dz, dy), (1, dy, dz)]
        now = [item for item in items if item not in [late for _, late in LATE]]
        now += [late for when, late in LATE if when == turn]
        return [reduce_item(*item) for item in now]


    def score_block(block, slot):
        keys = shards[block, HEAD_ROWS:, 0:DH]
        values = shards[block, HEAD_ROWS:, DH:]
        key_wide = jnp.concatenate([keys, ones], axis=1)
        value_wide = jnp.concatenate([values, ones], axis=1)
        sums = []
        following = contract_last(grad_wide[0], value_wide)
        for head in range(HEADS):
            span = slice(head * TOK, (head + 1) * TOK)
            prob_grad = following
            if head + 1 < HEADS:
                following = contract_last(grad_wide[head + 1], value_wide)
            score_grad = prob[me - block, span, :].astype(F32) * prob_grad
            low = score_grad.astype(BF16)
            folded = jnp.sum(low.astype(F32).reshape(TOK // 8, 8, TOK), axis=0)
            sums.append(jnp.sum(folded, axis=0, keepdims=True))
            score_low[slot, span, :] = low
            out_sum[head] += jnp.dot(low, key_wide, preferred_element_type=F32)
        columns = jnp.concatenate(sums + [jnp.zeros((4, TOK), F32)], axis=0)
        high = columns.astype(BF16).astype(F32)
        parts[block, 0:HEAD_ROWS, :] = jnp.concatenate([-high, high - columns], axis=0).astype(BF16)
        lane = lax.broadcasted_iota(jnp.int32, (8, DH), 1)
        whole = jnp.broadcast_to(jnp.sum(columns, axis=1, keepdims=True), (8, DH))
        offset[...] += jnp.where((lane >= block) & (lane < me), whole, 0.0)

    def product_block(block, slot):
        key_part = jnp.dot(query_turned[...], score_low[slot], preferred_element_type=F32) * LN2
        value_part = jnp.dot(grad_turned[...], prob[me - block], preferred_element_type=F32)
        parts[block, HEAD_ROWS : HEAD_ROWS + DH, :] = key_part.astype(BF16)
        parts[block, HEAD_ROWS + DH :, :] = value_part.astype(BF16)

    def block_of(cell, which):
        block = cell * 2 + jnp.where(which == 1, core, 1 - core)
        return block, (block <= me) & (block >= me - BACK)

    def small_copies(axis):
        return [
            remote(small.at[axis], small_landed.at[7 * axis + i], small_send, small_recv, 7 * axis + i, device)
            for i, device in enumerate(partners[axis])
        ]

    def small_add(axis):
        whole = small[axis]
        shared = lax.broadcasted_iota(jnp.int32, (16, DH), 0) < 8
        for i, made in enumerate(small_copies(axis)):
            made.wait_recv()
            term = small_landed[7 * axis + i]
            if axis == 1 and field_steps[i][1]:
                term = jnp.where(shared, term, 0.0)
            whole = whole + term
        small[axis + 1] = whole

    def backward_step(held, turn, _):
        step = STEPS - 1 - turn
        cell = chip_of(step, ORDER)

        def one(which, _):
            block, used = block_of(cell, which)
            slot = step * 2 + which if held else 0

            @pl.when(used)
            def _():
                if not held:
                    score_block(block, slot)
                product_block(block, slot)

            @pl.when(jnp.logical_not(used))
            def _():
                parts[block] = jnp.zeros((ROWS, 2 * DH), BF16)

            @pl.when(which == 0)
            def _():
                twin_copy(step, block, cell).start()

            return 0

        lax.fori_loop(0, 2, one, 0)
        first = STEPS - HELD
        for at in range(first + 1, STEPS) if held else range(1, first):

            @pl.when(turn == at)
            def _():
                reduce_turn(at)
                if at == STEPS - 2:
                    small_add(0)
                    for made in small_copies(1):
                        made.start()

        return 0

    def held_step(step, _):
        cell = chip_of(step, ORDER)

        def one(which, _):
            block, used = block_of(cell, which)

            @pl.when(used)
            def _():
                score_block(block, step * 2 + which)

            return 0

        return lax.fori_loop(0, 2, one, 0)

    lax.fori_loop(0, STEPS - HELD, functools.partial(backward_step, False), 0)
    lax.fori_loop(0, HELD, held_step, 0)
    reduce_turn(STEPS - HELD)


    query_gain_sum = jnp.zeros((1, DH), F32)
    turned = []
    for head in range(HEADS):
        span = slice(head * DH, (head + 1) * DH)
        raw = query_ref[:, span].astype(F32)
        scale = lax.rsqrt(jnp.mean(raw * raw, axis=1, keepdims=True) + EPS)
        hat = raw * scale
        cotangent = out_sum[head, :, 0:DH]
        query_gain_sum += jnp.sum(cotangent * hat, axis=0, keepdims=True)
        inner = cotangent * query_scale
        mean = jnp.mean(inner * hat, axis=1, keepdims=True)
        query_grad_ref[:, span] = (scale * (inner - hat * mean)).astype(BF16)
        halves = [jnp.transpose(out_sum[head, half * DH : (half + 1) * DH, DH:])[0:1] for half in (0, 1)]
        turned.append(jnp.concatenate(halves, axis=1))
    row_sums[...] = jnp.concatenate(turned, axis=0)
    query_gain_sum = query_gain_sum * (DH**-0.5)
    key_gain_row = query_gain_sum * query_gain_ref[...] / key_gain_ref[...]
    small[0] = jnp.concatenate(
        [query_gain_sum, key_gain_row, jnp.zeros((6, DH), F32), offset[...]], axis=0
    )

    for made in small_copies(0):
        made.start()
    lax.fori_loop(STEPS - HELD, STEPS, functools.partial(backward_step, True), 0)
    finals = reduce_turn(STEPS)

    value_grad_ref[...] = turn(finals[1]).astype(BF16)
    cotangent = turn(finals[0][HEAD_ROWS:])
    raw = key_ref[...].astype(F32)
    scale = lax.rsqrt(jnp.mean(raw * raw, axis=1, keepdims=True) + EPS)
    hat = raw * scale
    inner = cotangent * key_gain_ref[...]
    mean = jnp.mean(inner * hat, axis=1, keepdims=True)
    key_grad_ref[...] = (scale * (inner - hat * mean)).astype(BF16)

    gates = finals[0][0:4] + finals[0][8:12] + row_sums[...]
    row = lax.broadcasted_iota(jnp.int32, (TOK, TOK), 0)
    col = lax.broadcasted_iota(jnp.int32, (TOK, TOK), 1)
    lower = (row >= col).astype(F32)
    suffix = jnp.dot(gates, lower, preferred_element_type=F32, precision=lax.Precision.HIGHEST)
    logit = logit_ref[...].astype(F32)
    small_add(1)
    lane = lax.broadcasted_iota(jnp.int32, (4, DH), 1)
    later = jnp.sum(jnp.where(lane == me, small[2, 8:12, :], 0.0), axis=1, keepdims=True)
    forget_grad_ref[...] = (suffix + later) / (1.0 + jnp.exp(logit))
    gain_out_ref[...] = small[2, 0:2, :]

    for number, tree, part in sent:
        place = shards.at[0, rows_of(tree, part)]
        remote(place, place, out_send, out_recv, number, sibling).wait_send()
    for number, tree, name, part in back:
        goal = land(tree, name, part)
        remote(goal, goal, back_send, back_recv, number, sibling).wait_send()
    for at in range(STEPS):
        twin_copy(at, 0, 0).wait_send()
    for axis in range(2):
        for made in sum_copies(axis) + small_copies(axis):
            made.wait_send()


def fused(lengths_row, key_local, value_local, logit_local, query_local, grad_local, query_gain, key_gain):
    vmem = pl.BlockSpec(memory_space=pltpu.VMEM)
    smem = pl.BlockSpec(memory_space=pltpu.SMEM)
    wide = jax.ShapeDtypeStruct((TOK, HEADS * DH), BF16)
    narrow = jax.ShapeDtypeStruct((TOK, DH), BF16)
    rows = HEADS * TOK
    dma = pltpu.SemaphoreType.DMA
    return pl.pallas_call(
        fused_kernel,
        out_shape=(
            wide,
            wide,
            narrow,
            narrow,
            jax.ShapeDtypeStruct((HEADS, TOK), F32),
            jax.ShapeDtypeStruct((2, DH), F32),
        ),
        in_specs=[smem] + [vmem] * 7,
        out_specs=(vmem,) * 6,
        scratch_shapes=[
            pltpu.VMEM((SHARDS, ROWS, 2 * DH), BF16),
            pltpu.VMEM((4, 8, 8, DH), F32),
            pltpu.VMEM((SHARDS, 8, DH), F32),
            pltpu.VMEM((HEADS, TOK, 2 * DH), BF16),
            pltpu.VMEM((DH, rows), BF16),
            pltpu.VMEM((HEADS, TOK, 2 * DH), BF16),
            pltpu.VMEM((DH, rows), BF16),
            pltpu.VMEM((BACK + 1, rows, TOK), BF16),
            pltpu.VMEM((2 * HELD, rows, TOK), BF16),
            pltpu.VMEM((HEADS, TOK, 2 * DH), F32),
            pltpu.VMEM((8, DH), F32),
            pltpu.VMEM((HEADS, TOK), F32),
            pltpu.VMEM((SHARDS, ROWS, 2 * DH), BF16),
            pltpu.VMEM((SHARDS // 2, ROWS, 2 * DH), BF16),
            pltpu.VMEM((SHARDS // 2, ROWS, 2 * DH), BF16),
            pltpu.VMEM((40, PIECES[1][1], 2 * DH), BF16),
            pltpu.VMEM((3, 16, DH), F32),
            pltpu.VMEM((22, 16, DH), F32),
            dma((40 + 2 * STEPS,)),
            dma((40 + 2 * STEPS,)),
            dma((40 + STEPS,)),
            dma((40 + STEPS,)),
            dma((10,)),
            dma((10,)),
            dma((22,)),
            dma((22,)),
        ],
        compiler_params=pltpu.CompilerParams(
            collective_id=0, has_side_effects=True, vmem_limit_bytes=56 * 2**20
        ),
        name="attend_whole",
    )(lengths_row, key_local, value_local, logit_local, query_local, grad_local, query_gain, key_gain)


def write_kernel(*refs):
    count = len(refs) // 2
    for i in range(count):
        refs[count + i][...] = refs[i][...]


def write(*arrays):
    vmem = pl.BlockSpec(memory_space=pltpu.VMEM)
    return pl.pallas_call(
        write_kernel,
        out_shape=tuple(jax.ShapeDtypeStruct(a.shape, a.dtype) for a in arrays),
        in_specs=[vmem] * len(arrays),
        out_specs=(vmem,) * len(arrays),
        name="write_results",
    )(*arrays)


def on_device(queries, key_vectors, values, forget_logit, out_grad, query_gain, key_gain, lengths):
    results = fused(
        lengths[0],
        key_vectors[0],
        values[0],
        forget_logit[0],
        queries[0],
        out_grad[0],
        query_gain.reshape(1, DH),
        key_gain.reshape(1, DH),
    )
    attention, query_grad, key_grad, value_grad, forget_grad, gain_grad = write(*results)
    return (
        attention[None],
        query_grad[None],
        key_grad[None],
        value_grad[None],
        forget_grad[None],
        gain_grad,
    )


def solution(mesh):
    return jax.shard_map(
        on_device,
        mesh=mesh,
        in_specs=(
            P("rep", "seq", None),
            P("rep", "seq", None),
            P("rep", "seq", None),
            P("rep", None, "seq"),
            P("rep", "seq", None),
            P(),
            P(),
            P("rep", None),
        ),
        out_specs=(
            P("rep", "seq", None),
            P("rep", "seq", None),
            P("rep", "seq", None),
            P("rep", "seq", None),
            P("rep", None, "seq"),
            P(),
        ),
        check_vma=False,
    )
```
